512 devices in a mesh: row: 32 (over z, x), col: 16 (over y, core).
Axes of the slice: x: 4, y: 8, z: 8, core: 2. Of those that a mesh axis runs over, the one named last changes fastest.
Arguments:
- density: float32 [32, 256, 2048], P(None, 'row', 'col'), may hold values from 0 to 1
- threshold_index: int32 [3], replicated, may hold values from 4 to 12
- channel_width: int32 [30], replicated, may hold values from 0 to 9
- sigma_table: float32 [10], replicated, may hold values from 1.5 to 64
Outputs:
- compliance: float32 [30], replicated
- sensitivity: float32 [32, 256, 2048], P(None, 'row', 'col')
The draws below stay inside these ranges and needn't reach their ends.
All inputs are finite; a program needn't handle non-finite values.
Results may differ from the reference program's by a relative error of at most 0.0013.
Values may be sent and summed in bfloat16 or wider, within the bound.
No kernel may reach another device: no remote copies, remote signals or barrier semaphores. Data moves between devices by JAX's collectives and lax.ppermute only.
A program may use at most 64 MiB of HBM per device.

```python
import jax
import jax.numpy as jnp
from jax import lax

VARIANTS = 3
WIDTHS = 10
CHANNELS = 30
HALF = 128
NZ = 32
NY = 256
NX = 2048


def draw_density(key, part):
    first, second, third = jax.random.split(key, 3)
    base = jax.random.uniform(first, (NZ, NY, NX), jnp.float32)
    waves = jax.random.randint(second, (2,), 1, 4).astype(jnp.float32)
    phase = jax.random.uniform(third, (), jnp.float32, 0.0, 6.2831853)
    rows_pos = jnp.arange(NY).astype(jnp.float32)[:, None] / NY
    cols_pos = jnp.arange(NX).astype(jnp.float32)[None, :] / NX
    region = 0.55 + 0.45 * jnp.sin(6.2831853 * (waves[0] * rows_pos + waves[1] * cols_pos) + phase)
    return base * region[None, :, :]


def draw_sigma_table(key, part):
    first, second = jax.random.split(jax.random.fold_in(key, 17))
    lowest = 1.5
    highest = HALF / 2.0
    spots = (jnp.arange(WIDTHS).astype(jnp.float32) + jax.random.uniform(first, (WIDTHS,), jnp.float32)) / WIDTHS
    values = lowest * jnp.exp(spots * jnp.log(highest / lowest))
    values = jnp.minimum(values, highest)
    return jax.random.permutation(second, values)


def plant(drawn, own_key, smallest, top_value):
    index_at = [jax.random.randint(jax.random.fold_in(own_key, axis), (), 0, length) for axis, length in enumerate(drawn.shape)]
    longest = drawn.shape.index(max(drawn.shape))
    next_to = index_at[:longest] + [(index_at[longest] + 1) % drawn.shape[longest]] + index_at[longest + 1:]
    return drawn.at[tuple(index_at)].set(smallest).at[tuple(next_to)].set(top_value)


def setup_inputs(seed: int = 0) -> dict:
    streams_of = jax.random.split(jax.random.key(seed), 5)
    return {
        "density": draw_density(jax.random.fold_in(streams_of[4], 71), 0),
        "threshold_index": jax.random.randint(streams_of[1], (VARIANTS,), 4, 13).astype(jnp.int32),
        "channel_width": plant(jax.random.randint(streams_of[2], (CHANNELS,), 0, WIDTHS), jax.random.fold_in(streams_of[2], 1), 0, WIDTHS - 1).astype(jnp.int32),
        "sigma_table": draw_sigma_table(jax.random.fold_in(streams_of[4], 71), 0),
    }


sharpness = 8.0
spread_floor = 0.0001

def project(density, threshold_index):
    levels = threshold_index.astype(jnp.float32) / 16.0
    levels = levels.reshape((-1,) + (1,) * density.ndim)
    low = jnp.tanh(sharpness * levels)
    high = jnp.tanh(sharpness * (1.0 - levels))
    return (low + jnp.tanh(sharpness * (density - levels))) / (low + high)

def slope(density, threshold_index):
    levels = threshold_index.astype(jnp.float32) / 16.0
    levels = levels.reshape((-1,) + (1,) * density.ndim)
    low = jnp.tanh(sharpness * levels)
    high = jnp.tanh(sharpness * (1.0 - levels))
    inner = jnp.tanh(sharpness * (density - levels))
    return sharpness * (1.0 - inner * inner) / (low + high)

def taps_for(width_value):
    offsets = jnp.arange(-HALF, HALF + 1).astype(jnp.float32)
    inverse = 1.0 / jnp.sum(jnp.exp(-offsets * offsets / (2.0 * width_value * width_value)))
    rounded = (jnp.exp(-offsets * offsets / (2.0 * width_value * width_value)) * inverse).astype(jnp.bfloat16)
    return lax.optimization_barrier(rounded).astype(jnp.float32)

def smooth(field, taps, axis):
    length = field.shape[axis]
    total = length + 2 * HALF
    spectrum = jnp.fft.rfft(field, n=total, axis=axis)
    kernel = jnp.fft.rfft(taps, n=total)
    shape = [1] * field.ndim
    shape[axis] = -1
    result = jnp.fft.irfft(spectrum * kernel.reshape(shape), n=total, axis=axis)
    return lax.slice_in_dim(result, HALF, HALF + length, axis=axis).astype(jnp.float32)

def reference(density, threshold_index, channel_width, sigma_table):
    variants = lax.optimization_barrier(project(density, threshold_index).astype(jnp.bfloat16))

    def both_passes(index):
        variant = index // WIDTHS
        taps = taps_for(sigma_table[channel_width[index]])
        source = variants[variant].astype(jnp.float32)
        along = lax.optimization_barrier(smooth(source, taps, 2).astype(jnp.bfloat16)).astype(jnp.float32)
        return (smooth(along, taps, 1), source)

    def channel_sum(index):
        field, source = both_passes(index)
        return jnp.sum(field * source)
    channel_ids = jnp.arange(CHANNELS, dtype=jnp.int32)
    compliance = lax.map(channel_sum, channel_ids) / (NZ * NY * NX)
    mean_value = jnp.mean(compliance)
    spread = jnp.sqrt(jnp.mean((compliance - mean_value) ** 2) + spread_floor)
    weights = (1.0 + (compliance - mean_value) / spread) / CHANNELS

    def accumulate(index, combined):
        field, source = both_passes(index)
        variant = index // WIDTHS
        return combined.at[variant].add(2.0 * weights[index] * field)
    combined = lax.fori_loop(0, CHANNELS, accumulate, jnp.zeros((VARIANTS, NZ, NY, NX), jnp.float32))
    sensitivity = lax.optimization_barrier(jnp.sum(slope(density, threshold_index) * combined, axis=0))
    return (compliance, sensitivity)
```

```python
import jax
import jax.numpy as jnp
from jax import lax
from jax.experimental import pallas as pl
from jax.experimental.pallas import tpu as pltpu
from jax.sharding import PartitionSpec as P

VARIANTS = 3
WIDTHS = 10
CHANNELS = 30
HALF = 128
SHARPNESS = 8.0
SPREAD_FLOOR = 0.0001

F32 = jnp.float32
BF16 = jnp.bfloat16
VMEM = pl.BlockSpec(memory_space=pltpu.VMEM)
SMEM = pl.BlockSpec(memory_space=pltpu.SMEM)
MIB = 1024 * 1024


def bands_kernel(sigma_ref, width_ref, xt_ref, y_ref, member_ref):
    row = lax.broadcasted_iota(jnp.int32, (HALF, HALF), 0)
    col = lax.broadcasted_iota(jnp.int32, (HALF, HALF), 1)
    gap = col - row
    gap_f = gap.astype(F32)
    squares = ((gap_f - HALF) ** 2, gap_f * gap_f, (gap_f + HALF) ** 2)
    masks = (gap >= 0, None, gap <= 0)
    taps = lax.broadcasted_iota(jnp.int32, (1, HALF), 1).astype(F32) + 1.0
    for w in range(WIDTHS):
        sigma = jnp.full((1, HALF), sigma_ref[w], F32)
        scale = -1.0 / (2.0 * sigma * sigma)
        total = 1.0 + 2.0 * jnp.sum(jnp.exp(taps * taps * scale), axis=1, keepdims=True)
        inverse = 1.0 / total
        blocks = []
        for square, mask in zip(squares, masks):
            value = jnp.exp(square * scale) * inverse
            if mask is not None:
                value = jnp.where(mask, value, 0.0)
            blocks.append(value.astype(BF16))
        before, middle, after = blocks
        rows = slice(w * HALF, (w + 1) * HALF)
        xt_ref[rows, 0:HALF] = before
        xt_ref[rows, HALF : 2 * HALF] = middle
        xt_ref[rows, 2 * HALF : 3 * HALF] = after
        y_ref[w, 0:HALF, 0:HALF] = middle
        y_ref[w, 0:HALF, HALF : 2 * HALF] = after
        y_ref[w, HALF : 2 * HALF, 0:HALF] = before
        y_ref[w, HALF : 2 * HALF, HALF : 2 * HALF] = middle
    lane = lax.broadcasted_iota(jnp.int32, (1, 128), 1)
    for c in range(CHANNELS):
        pair = (c // WIDTHS) * WIDTHS + width_ref[c]
        member_ref[c : c + 1, :] = (lane == pair).astype(F32)
    member_ref[CHANNELS:32, :] = jnp.zeros((32 - CHANNELS, 128), F32)


def column_to_row(column):
    rows = column.shape[0]
    at = lax.broadcasted_iota(jnp.int32, (rows, 128), 0) == lax.broadcasted_iota(jnp.int32, (rows, 128), 1)
    return jnp.sum(jnp.where(at, jnp.broadcast_to(column, (rows, 128)), 0.0), axis=0, keepdims=True)


def smooth_kernel(index_ref, left_ref, own_ref, right_ref, xt_ref, y_ref, t_ref, s_ref, part_ref, p_ref, own_p_ref, a_ref, rows_ref):
    ny = own_ref.shape[0]
    sides = (left_ref[...].T, own_ref[...].T, right_ref[...].T)
    for v in range(VARIANTS):
        level = jnp.full((1, ny), index_ref[v].astype(F32) * (1.0 / 16.0), F32)
        low = jnp.tanh(SHARPNESS * level)
        high = jnp.tanh(SHARPNESS * (1.0 - level))
        inverse = 1.0 / (low + high)
        for b, side in enumerate(sides):
            inner = jnp.tanh(SHARPNESS * (side - level))
            value = ((low + inner) * inverse).astype(BF16)
            p_ref[b * HALF : (b + 1) * HALF, :] = value
            if b == 1:
                own_p_ref[v] = value.astype(F32)
                s_ref[v] = SHARPNESS * (1.0 - inner * inner) * inverse
        along = jnp.dot(xt_ref[...], p_ref[...], preferred_element_type=F32).astype(BF16)
        a_ref[:, v * HALF : (v + 1) * HALF, :] = along.reshape(WIDTHS, HALF, ny)
    rows_ref[...] = jnp.zeros_like(rows_ref)

    def per_width(w, carry):
        field = jnp.dot(a_ref[w], y_ref[w], preferred_element_type=F32)
        t_ref[w] = field
        for v in range(VARIANTS):
            product = field[v * HALF : (v + 1) * HALF, :] * own_p_ref[v]
            line = jnp.sum(product, axis=0, keepdims=True)
            rows_ref[pl.ds(v * WIDTHS + w, 1), :] = line[:, 0:128] + line[:, 128:256]
        return carry

    lax.fori_loop(0, WIDTHS, per_width, 0)
    sums = column_to_row(jnp.sum(rows_ref[...], axis=1, keepdims=True))
    part_ref[...] = jnp.broadcast_to(sums.reshape(1, 1, 128), part_ref.shape)


def gather_kernel(in_ref, out_ref):
    total = jnp.sum(in_ref[...], axis=0, keepdims=True)
    out_ref[...] = jnp.broadcast_to(total, out_ref.shape)


def combine_kernel(cells, sums_ref, member_ref, t_ref, s_ref, compliance_ref, out_ref):
    pairs = jnp.sum(sums_ref[...], axis=0) * (1.0 / cells)
    member = member_ref[...]
    compliance = jnp.sum(member * pairs, axis=1, keepdims=True)
    valid = lax.broadcasted_iota(jnp.int32, (32, 1), 0) < CHANNELS
    mean = jnp.sum(compliance, axis=0, keepdims=True) * (1.0 / CHANNELS)
    away = jnp.where(valid, compliance - mean, 0.0)
    spread = jnp.sqrt(jnp.sum(away * away, axis=0, keepdims=True) * (1.0 / CHANNELS) + SPREAD_FLOOR)
    weight = (1.0 + away / spread) * (2.0 / CHANNELS)
    per_pair = jnp.sum(member * weight, axis=0, keepdims=True)
    compliance_ref[...] = column_to_row(compliance)
    total = None
    for v in range(VARIANTS):
        combined = None
        for w in range(WIDTHS):
            k = v * WIDTHS + w
            term = per_pair[:, k : k + 1] * t_ref[w, v * HALF : (v + 1) * HALF, :]
            combined = term if combined is None else combined + term
        combined = combined * s_ref[v]
        total = combined if total is None else total + combined
    out_ref[...] = total.T


def per_device(density, threshold_index, channel_width, sigma_table):
    planes, own_rows, nx = density.shape
    rows, cols = lax.axis_size("row"), lax.axis_size("col")
    ny = own_rows * rows
    cells = float(planes * ny * nx * cols)
    params = pltpu.CompilerParams(vmem_limit_bytes=24 * MIB)

    xt, y, member = pl.pallas_call(
        bands_kernel,
        out_shape=(
            jax.ShapeDtypeStruct((WIDTHS * HALF, 3 * HALF), BF16),
            jax.ShapeDtypeStruct((WIDTHS, ny, ny), BF16),
            jax.ShapeDtypeStruct((32, 128), F32),
        ),
        in_specs=[SMEM, SMEM],
        out_specs=[VMEM] * 3,
        compiler_params=params,
        cost_estimate=pl.CostEstimate(flops=10_000_000, bytes_accessed=2_500_000, transcendentals=500_000),
        name="bands",
    )(sigma_table, channel_width)

    plane = lax.all_to_all(density, "row", split_axis=0, concat_axis=0, tiled=True).reshape(ny, nx)
    up = [(i, i + 1) for i in range(cols - 1)]
    down = [(i + 1, i) for i in range(cols - 1)]
    left = lax.ppermute(plane, "col", up)
    right = lax.ppermute(plane, "col", down)

    t, s, part = pl.pallas_call(
        smooth_kernel,
        out_shape=(
            jax.ShapeDtypeStruct((WIDTHS, VARIANTS * HALF, ny), F32),
            jax.ShapeDtypeStruct((VARIANTS, HALF, ny), F32),
            jax.ShapeDtypeStruct((rows, 1, 128), F32),
        ),
        in_specs=[SMEM] + [VMEM] * 5,
        out_specs=[VMEM] * 3,
        scratch_shapes=[
            pltpu.VMEM((3 * HALF, ny), BF16),
            pltpu.VMEM((VARIANTS, HALF, ny), F32),
            pltpu.VMEM((WIDTHS, VARIANTS * HALF, ny), BF16),
            pltpu.VMEM((32, 128), F32),
        ],
        compiler_params=params,
        cost_estimate=pl.CostEstimate(flops=1_300_000_000, bytes_accessed=7_000_000, transcendentals=300_000),
        name="smooth",
    )(threshold_index, left, plane, right, xt, y)

    part = lax.all_to_all(part, "row", split_axis=0, concat_axis=0, tiled=True)
    part = pl.pallas_call(
        gather_kernel,
        out_shape=jax.ShapeDtypeStruct((cols, 1, 128), F32),
        in_specs=[VMEM],
        out_specs=VMEM,
        compiler_params=params,
        name="regroup",
    )(part)
    part = lax.all_to_all(part, "col", split_axis=0, concat_axis=0, tiled=True)

    compliance, sensitivity = pl.pallas_call(
        lambda *refs: combine_kernel(cells, *refs),
        out_shape=(
            jax.ShapeDtypeStruct((1, 128), F32),
            jax.ShapeDtypeStruct((ny, nx), F32),
        ),
        in_specs=[VMEM] * 4,
        out_specs=[VMEM] * 2,
        compiler_params=params,
        name="combine",
    )(part, member, t, s)
    sensitivity = lax.all_to_all(
        sensitivity.reshape(planes, own_rows, nx), "row", split_axis=0, concat_axis=0, tiled=True
    )
    return compliance[0, :CHANNELS], sensitivity


def solution(mesh):
    in_specs = (P(None, "row", "col"), P(), P(), P())
    out_specs = (P(), P(None, "row", "col"))
    return jax.shard_map(
        per_device, mesh=mesh, in_specs=in_specs, out_specs=out_specs, check_vma=False
    )
```

```python
import jax
import jax.numpy as jnp
from jax import lax
from jax.experimental import pallas as pl
from jax.experimental.pallas import tpu as pltpu
from jax.sharding import PartitionSpec as P

VARIANTS = 3
WIDTHS = 10
CHANNELS = 30
HALF = 128
SHARPNESS = 8.0
SPREAD_FLOOR = 0.0001

F32 = jnp.float32
BF16 = jnp.bfloat16
VMEM = pl.BlockSpec(memory_space=pltpu.VMEM)
SMEM = pl.BlockSpec(memory_space=pltpu.SMEM)
MIB = 1024 * 1024


def bands_kernel(sigma_ref, width_ref, index_ref, xt_ref, member_ref, level_ref):
    row = lax.broadcasted_iota(jnp.int32, (HALF, HALF), 0)
    col = lax.broadcasted_iota(jnp.int32, (HALF, HALF), 1)
    gap = col - row
    gap_f = gap.astype(F32)
    squares = ((gap_f - HALF) ** 2, gap_f * gap_f, (gap_f + HALF) ** 2)
    masks = (gap >= 0, None, gap <= 0)
    taps = lax.broadcasted_iota(jnp.int32, (1, HALF), 1).astype(F32) + 1.0
    for w in range(WIDTHS):
        sigma = jnp.full((1, HALF), sigma_ref[w], F32)
        scale = -1.0 / (2.0 * sigma * sigma)
        total = 1.0 + 2.0 * jnp.sum(jnp.exp(taps * taps * scale), axis=1, keepdims=True)
        inverse = 1.0 / total
        blocks = []
        for square, mask in zip(squares, masks):
            value = jnp.exp(square * scale) * inverse
            if mask is not None:
                value = jnp.where(mask, value, 0.0)
            blocks.append(value.astype(BF16))
        before, middle, after = blocks
        rows = slice(w * HALF, (w + 1) * HALF)
        xt_ref[rows, 0:HALF] = before
        xt_ref[rows, HALF : 2 * HALF] = middle
        xt_ref[rows, 2 * HALF : 3 * HALF] = after
    lane = lax.broadcasted_iota(jnp.int32, (1, 128), 1)
    for c in range(CHANNELS):
        pair = (c // WIDTHS) * WIDTHS + width_ref[c]
        member_ref[c : c + 1, :] = (lane == pair).astype(F32)
    member_ref[CHANNELS:32, :] = jnp.zeros((32 - CHANNELS, 128), F32)
    for v in range(VARIANTS):
        level = jnp.full((1, 128), index_ref[v].astype(F32) * (1.0 / 16.0), F32)
        low = jnp.tanh(SHARPNESS * level)
        high = jnp.tanh(SHARPNESS * (1.0 - level))
        level_ref[v : v + 1, :] = level
        level_ref[8 + v : 9 + v, :] = low
        level_ref[16 + v : 17 + v, :] = 1.0 / (low + high)


def column_to_row(column):
    rows = column.shape[0]
    at = lax.broadcasted_iota(jnp.int32, (rows, 128), 0) == lax.broadcasted_iota(jnp.int32, (rows, 128), 1)
    return jnp.sum(jnp.where(at, jnp.broadcast_to(column, (rows, 128)), 0.0), axis=0, keepdims=True)


def constants(level_ref, v, width):
    rows = [level_ref[8 * i + v : 8 * i + v + 1, :] for i in range(3)]
    return [jnp.concatenate([row] * (width // 128), axis=1) for row in rows]


def project(side, level, low, inverse):
    inner = jnp.tanh(SHARPNESS * (side - level))
    return ((low + inner) * inverse).astype(BF16), inner


def square_band(xt_ref, w):
    rows = pl.ds(w * HALF, HALF)
    return jnp.concatenate([xt_ref[rows, HALF : 3 * HALF], xt_ref[rows, 0 : 2 * HALF]], axis=0)


def own_kernel(own_ref, xt_ref, level_ref, b_ref, rows_ref, p_ref, a_ref):
    ny = own_ref.shape[0]
    own = own_ref[...].T
    for v in range(VARIANTS):
        level, low, inverse = constants(level_ref, v, ny)
        value, _ = project(own, level, low, inverse)
        p_ref[v * HALF : (v + 1) * HALF, :] = value
        along = jnp.dot(xt_ref[:, HALF : 2 * HALF], value, preferred_element_type=F32)
        a_ref[:, v * HALF : (v + 1) * HALF, :] = along.reshape(WIDTHS, HALF, ny)
    rows_ref[...] = jnp.zeros_like(rows_ref)

    def per_width(w, carry):
        b = jnp.dot(p_ref[...], square_band(xt_ref, w), preferred_element_type=F32)
        b_ref[w] = b
        product = a_ref[w] * b
        for v in range(VARIANTS):
            line = jnp.sum(product[v * HALF : (v + 1) * HALF, :], axis=0, keepdims=True)
            rows_ref[pl.ds(v * WIDTHS + w, 1), :] = line[:, 0:128] + line[:, 128:256]
        return carry

    lax.fori_loop(0, WIDTHS, per_width, 0)


def cross_kernel(right_ref, xt_ref, level_ref, b_ref, own_rows_ref, part_ref, rows_ref):
    ny = right_ref.shape[0]
    right = right_ref[...].T
    rows_ref[...] = own_rows_ref[...]
    for v in range(VARIANTS):
        level, low, inverse = constants(level_ref, v, ny)
        value, _ = project(right, level, low, inverse)
        along = jnp.dot(xt_ref[:, 2 * HALF : 3 * HALF], value, preferred_element_type=F32)
        for w in range(WIDTHS):
            product = along[w * HALF : (w + 1) * HALF, :] * b_ref[w, v * HALF : (v + 1) * HALF, :]
            line = jnp.sum(product, axis=0, keepdims=True)
            k = v * WIDTHS + w
            rows_ref[k : k + 1, :] += 2.0 * (line[:, 0:128] + line[:, 128:256])
    sums = column_to_row(jnp.sum(rows_ref[...], axis=1, keepdims=True))
    part_ref[...] = jnp.broadcast_to(sums.reshape(1, 1, 128), part_ref.shape)


def along_kernel(left_ref, own_ref, right_ref, xt_ref, level_ref, a_ref, p_ref):
    ny = left_ref.shape[0]
    left, own, right = left_ref[...].T, own_ref[...].T, right_ref[...].T
    for v in range(VARIANTS):
        level, low, inverse = constants(level_ref, v, ny)
        p_ref[0:HALF, :] = project(left, level, low, inverse)[0]
        p_ref[HALF : 2 * HALF, :] = project(own, level, low, inverse)[0]
        p_ref[2 * HALF : 3 * HALF, :] = project(right, level, low, inverse)[0]
        along = jnp.dot(xt_ref[...], p_ref[...], preferred_element_type=F32).astype(BF16)
        a_ref[:, v * HALF : (v + 1) * HALF, :] = along.reshape(WIDTHS, HALF, ny)


def gather_kernel(in_ref, out_ref):
    total = jnp.sum(in_ref[...], axis=0, keepdims=True)
    out_ref[...] = jnp.broadcast_to(total, out_ref.shape)


def combine_kernel(cells, sums_ref, member_ref, a_ref, own_ref, xt_ref, level_ref, compliance_ref, out_ref, total_ref):
    pairs = jnp.sum(sums_ref[...], axis=0) * (1.0 / cells)
    member = member_ref[...]
    compliance = jnp.sum(member * pairs, axis=1, keepdims=True)
    valid = lax.broadcasted_iota(jnp.int32, (32, 1), 0) < CHANNELS
    mean = jnp.sum(compliance, axis=0, keepdims=True) * (1.0 / CHANNELS)
    away = jnp.where(valid, compliance - mean, 0.0)
    spread = jnp.sqrt(jnp.sum(away * away, axis=0, keepdims=True) * (1.0 / CHANNELS) + SPREAD_FLOOR)
    weight = (1.0 + away / spread) * (2.0 / CHANNELS)
    per_pair = jnp.sum(member * weight, axis=0, keepdims=True)
    compliance_ref[...] = column_to_row(compliance)[0, :CHANNELS]
    for w in range(WIDTHS):
        field = jnp.dot(a_ref[w], square_band(xt_ref, w), preferred_element_type=F32)
        for v in range(VARIANTS):
            k = v * WIDTHS + w
            term = per_pair[:, k : k + 1] * field[v * HALF : (v + 1) * HALF, :]
            total_ref[v] = term if w == 0 else total_ref[v] + term
    own = own_ref[...].T
    total = None
    for v in range(VARIANTS):
        level, low, inverse = constants(level_ref, v, own.shape[1])
        inner = jnp.tanh(SHARPNESS * (own - level))
        term = total_ref[v] * (SHARPNESS * (1.0 - inner * inner) * inverse)
        total = term if total is None else total + term
    out_ref[...] = total.T


def call(kernel, name, out, inputs, scratch=(), specs=None, flops=0, moved=0, special=0):
    return pl.pallas_call(
        kernel,
        out_shape=tuple(jax.ShapeDtypeStruct(shape, dtype) for shape, dtype in out),
        in_specs=specs or [VMEM] * len(inputs),
        out_specs=(VMEM,) * len(out),
        scratch_shapes=list(scratch),
        compiler_params=pltpu.CompilerParams(vmem_limit_bytes=24 * MIB),
        cost_estimate=pl.CostEstimate(flops=flops, bytes_accessed=moved, transcendentals=special),
        name=name,
    )(*inputs)


def per_device(density, threshold_index, channel_width, sigma_table):
    planes, own_rows, nx = density.shape
    rows, cols = lax.axis_size("row"), lax.axis_size("col")
    ny = own_rows * rows
    cells = float(planes * ny * nx * cols)
    tall = VARIANTS * HALF

    xt, member, levels = call(
        bands_kernel,
        "bands",
        (((WIDTHS * HALF, 3 * HALF), BF16), ((32, 128), F32), ((24, 128), F32)),
        (sigma_table, channel_width, threshold_index),
        specs=[SMEM] * 3,
        flops=10_000_000,
        moved=2_500_000,
        special=500_000,
    )
    plane = lax.all_to_all(density, "row", split_axis=0, concat_axis=0, tiled=True).reshape(ny, nx)
    plane, xt, member, levels = lax.optimization_barrier((plane, xt, member, levels))
    right = lax.ppermute(plane, "col", [(i + 1, i) for i in range(cols - 1)])

    b, own_rows_sum = call(
        own_kernel,
        "own",
        (((WIDTHS, tall, ny), F32), ((32, 128), F32)),
        (plane, xt, levels),
        scratch=(pltpu.VMEM((tall, ny), BF16), pltpu.VMEM((WIDTHS, tall, ny), F32)),
        flops=750_000_000,
        moved=7_000_000,
        special=100_000,
    )
    (part,) = call(
        cross_kernel,
        "cross",
        (((rows, 1, 128), F32),),
        (right, xt, levels, b, own_rows_sum),
        scratch=(pltpu.VMEM((32, 128), F32),),
        flops=250_000_000,
        moved=5_000_000,
        special=100_000,
    )
    later, part = lax.optimization_barrier((plane, part))
    left = lax.ppermute(later, "col", [(i, i + 1) for i in range(cols - 1)])
    part = lax.all_to_all(part, "row", split_axis=0, concat_axis=0, tiled=True)
    (part,) = call(gather_kernel, "regroup", (((cols, 1, 128), F32),), (part,))
    part = lax.all_to_all(part, "col", split_axis=0, concat_axis=0, tiled=True)

    (a,) = call(
        along_kernel,
        "along",
        (((WIDTHS, tall, ny), BF16),),
        (left, plane, right, xt, levels),
        scratch=(pltpu.VMEM((3 * HALF, ny), BF16),),
        flops=800_000_000,
        moved=4_000_000,
        special=300_000,
    )
    compliance, sensitivity = call(
        lambda *refs: combine_kernel(cells, *refs),
        "combine",
        (((CHANNELS,), F32), ((ny, nx), F32)),
        (part, member, a, plane, xt, levels),
        scratch=(pltpu.VMEM((VARIANTS, HALF, ny), F32),),
        flops=500_000_000,
        moved=5_000_000,
    )
    sensitivity = lax.all_to_all(
        sensitivity.reshape(planes, own_rows, nx), "row", split_axis=0, concat_axis=0, tiled=True
    )
    return compliance, sensitivity


def solution(mesh):
    in_specs = (P(None, "row", "col"), P(), P(), P())
    out_specs = (P(), P(None, "row", "col"))
    return jax.shard_map(
        per_device, mesh=mesh, in_specs=in_specs, out_specs=out_specs, check_vma=False
    )
```

```python
import jax
import jax.numpy as jnp
from jax import lax
from jax.experimental import pallas as pl
from jax.experimental.pallas import tpu as pltpu
from jax.sharding import PartitionSpec as P

VARIANTS = 3
WIDTHS = 10
CHANNELS = 30
HALF = 128
SHARPNESS = 8.0
SPREAD_FLOOR = 0.0001

F32 = jnp.float32
BF16 = jnp.bfloat16
VMEM = pl.BlockSpec(memory_space=pltpu.VMEM)
SMEM = pl.BlockSpec(memory_space=pltpu.SMEM)
MIB = 1024 * 1024


def bands_kernel(sigma_ref, width_ref, index_ref, xt_ref, member_ref, level_ref):
    row = lax.broadcasted_iota(jnp.int32, (HALF, HALF), 0)
    col = lax.broadcasted_iota(jnp.int32, (HALF, HALF), 1)
    gap = col - row
    gap_f = gap.astype(F32)
    squares = ((gap_f - HALF) ** 2, gap_f * gap_f, (gap_f + HALF) ** 2)
    masks = (gap >= 0, None, gap <= 0)
    taps = lax.broadcasted_iota(jnp.int32, (1, HALF), 1).astype(F32) + 1.0
    for w in range(WIDTHS):
        sigma = jnp.full((1, HALF), sigma_ref[w], F32)
        scale = -1.0 / (2.0 * sigma * sigma)
        total = 1.0 + 2.0 * jnp.sum(jnp.exp(taps * taps * scale), axis=1, keepdims=True)
        inverse = 1.0 / total
        blocks = []
        for square, mask in zip(squares, masks):
            value = jnp.exp(square * scale) * inverse
            if mask is not None:
                value = jnp.where(mask, value, 0.0)
            blocks.append(value.astype(BF16))
        before, middle, after = blocks
        rows = slice(w * HALF, (w + 1) * HALF)
        xt_ref[rows, 0:HALF] = before
        xt_ref[rows, HALF : 2 * HALF] = middle
        xt_ref[rows, 2 * HALF : 3 * HALF] = after
    lane = lax.broadcasted_iota(jnp.int32, (1, 128), 1)
    for c in range(CHANNELS):
        pair = (c // WIDTHS) * WIDTHS + width_ref[c]
        member_ref[c : c + 1, :] = (lane == pair).astype(F32)
    member_ref[CHANNELS:32, :] = jnp.zeros((32 - CHANNELS, 128), F32)
    for v in range(VARIANTS):
        level = jnp.full((1, 128), index_ref[v].astype(F32) * (1.0 / 16.0), F32)
        low = jnp.tanh(SHARPNESS * level)
        high = jnp.tanh(SHARPNESS * (1.0 - level))
        level_ref[v : v + 1, :] = level
        level_ref[8 + v : 9 + v, :] = low
        level_ref[16 + v : 17 + v, :] = 1.0 / (low + high)


def column_to_row(column):
    rows = column.shape[0]
    at = lax.broadcasted_iota(jnp.int32, (rows, 128), 0) == lax.broadcasted_iota(jnp.int32, (rows, 128), 1)
    return jnp.sum(jnp.where(at, jnp.broadcast_to(column, (rows, 128)), 0.0), axis=0, keepdims=True)


def constants(level_ref, v, width):
    rows = [level_ref[8 * i + v : 8 * i + v + 1, :] for i in range(3)]
    return [jnp.concatenate([row] * (width // 128), axis=1) for row in rows]


def project(side, level, low, inverse):
    inner = jnp.tanh(SHARPNESS * (side - level))
    return ((low + inner) * inverse).astype(BF16), inner


def square_band(xt_ref, w):
    rows = pl.ds(w * HALF, HALF)
    return jnp.concatenate([xt_ref[rows, HALF : 3 * HALF], xt_ref[rows, 0 : 2 * HALF]], axis=0)


def own_kernel(own_ref, xt_ref, level_ref, b_ref, rows_ref, p_ref, a_ref):
    ny = own_ref.shape[0]
    own = own_ref[...].T
    for v in range(VARIANTS):
        level, low, inverse = constants(level_ref, v, ny)
        value, _ = project(own, level, low, inverse)
        p_ref[v * HALF : (v + 1) * HALF, :] = value
    rows_ref[...] = jnp.zeros_like(rows_ref)
    for v in range(VARIANTS):
        part = p_ref[v * HALF : (v + 1) * HALF, :]
        along = jnp.dot(xt_ref[:, HALF : 2 * HALF], part, preferred_element_type=F32)
        a_ref[:, v * HALF : (v + 1) * HALF, :] = along.reshape(WIDTHS, HALF, ny)
    for w in range(WIDTHS):
        b = jnp.dot(p_ref[...], square_band(xt_ref, w), preferred_element_type=F32)
        b_ref[w] = b
        product = a_ref[w] * b
        for v in range(VARIANTS):
            line = jnp.sum(product[v * HALF : (v + 1) * HALF, :], axis=0, keepdims=True)
            rows_ref[v * WIDTHS + w : v * WIDTHS + w + 1, :] = line[:, 0:128] + line[:, 128:256]


def cross_kernel(right_ref, xt_ref, level_ref, b_ref, own_rows_ref, part_ref, rows_ref):
    ny = right_ref.shape[0]
    right = right_ref[...].T
    rows_ref[...] = own_rows_ref[...]
    for v in range(VARIANTS):
        level, low, inverse = constants(level_ref, v, ny)
        value, _ = project(right, level, low, inverse)
        along = jnp.dot(xt_ref[:, 2 * HALF : 3 * HALF], value, preferred_element_type=F32)
        for w in range(WIDTHS):
            product = along[w * HALF : (w + 1) * HALF, :] * b_ref[w, v * HALF : (v + 1) * HALF, :]
            line = jnp.sum(product, axis=0, keepdims=True)
            k = v * WIDTHS + w
            rows_ref[k : k + 1, :] += 2.0 * (line[:, 0:128] + line[:, 128:256])
    sums = column_to_row(jnp.sum(rows_ref[...], axis=1, keepdims=True))
    part_ref[...] = jnp.broadcast_to(sums.reshape(1, 1, 128), part_ref.shape)


def along_kernel(left_ref, own_ref, right_ref, xt_ref, level_ref, a_ref, p_ref):
    ny = left_ref.shape[0]
    left, own, right = left_ref[...].T, own_ref[...].T, right_ref[...].T
    for v in range(VARIANTS):
        level, low, inverse = constants(level_ref, v, ny)
        p_ref[0:HALF, :] = project(left, level, low, inverse)[0]
        p_ref[HALF : 2 * HALF, :] = project(own, level, low, inverse)[0]
        p_ref[2 * HALF : 3 * HALF, :] = project(right, level, low, inverse)[0]
        along = jnp.dot(xt_ref[...], p_ref[...], preferred_element_type=F32).astype(BF16)
        a_ref[:, v * HALF : (v + 1) * HALF, :] = along.reshape(WIDTHS, HALF, ny)


def gather_kernel(in_ref, out_ref):
    total = jnp.sum(in_ref[...], axis=0, keepdims=True)
    out_ref[...] = jnp.broadcast_to(total, out_ref.shape)


def combine_kernel(cells, sums_ref, member_ref, a_ref, own_ref, xt_ref, level_ref, compliance_ref, out_ref, total_ref):
    pairs = jnp.sum(sums_ref[...], axis=0) * (1.0 / cells)
    member = member_ref[...]
    compliance = jnp.sum(member * pairs, axis=1, keepdims=True)
    valid = lax.broadcasted_iota(jnp.int32, (32, 1), 0) < CHANNELS
    mean = jnp.sum(compliance, axis=0, keepdims=True) * (1.0 / CHANNELS)
    away = jnp.where(valid, compliance - mean, 0.0)
    spread = jnp.sqrt(jnp.sum(away * away, axis=0, keepdims=True) * (1.0 / CHANNELS) + SPREAD_FLOOR)
    weight = (1.0 + away / spread) * (2.0 / CHANNELS)
    per_pair = jnp.sum(member * weight, axis=0, keepdims=True)
    compliance_ref[...] = column_to_row(compliance)[0, :CHANNELS]
    for w in range(WIDTHS):
        field = jnp.dot(a_ref[w], square_band(xt_ref, w), preferred_element_type=F32)
        for v in range(VARIANTS):
            k = v * WIDTHS + w
            term = per_pair[:, k : k + 1] * field[v * HALF : (v + 1) * HALF, :]
            total_ref[v] = term if w == 0 else total_ref[v] + term
    own = own_ref[...].T
    total = None
    for v in range(VARIANTS):
        level, low, inverse = constants(level_ref, v, own.shape[1])
        inner = jnp.tanh(SHARPNESS * (own - level))
        term = total_ref[v] * (SHARPNESS * (1.0 - inner * inner) * inverse)
        total = term if total is None else total + term
    out_ref[...] = total.T


def call(kernel, name, out, inputs, scratch=(), specs=None, flops=0, moved=0, special=0):
    return pl.pallas_call(
        kernel,
        out_shape=tuple(jax.ShapeDtypeStruct(shape, dtype) for shape, dtype in out),
        in_specs=specs or [VMEM] * len(inputs),
        out_specs=(VMEM,) * len(out),
        scratch_shapes=list(scratch),
        compiler_params=pltpu.CompilerParams(vmem_limit_bytes=24 * MIB),
        cost_estimate=pl.CostEstimate(flops=flops, bytes_accessed=moved, transcendentals=special),
        name=name,
    )(*inputs)


def per_device(density, threshold_index, channel_width, sigma_table):
    planes, own_rows, nx = density.shape
    rows, cols = lax.axis_size("row"), lax.axis_size("col")
    ny = own_rows * rows
    cells = float(planes * ny * nx * cols)
    tall = VARIANTS * HALF

    xt, member, levels = call(
        bands_kernel,
        "bands",
        (((WIDTHS * HALF, 3 * HALF), BF16), ((32, 128), F32), ((24, 128), F32)),
        (sigma_table, channel_width, threshold_index),
        specs=[SMEM] * 3,
        flops=10_000_000,
        moved=2_500_000,
        special=500_000,
    )
    plane = lax.all_to_all(density, "row", split_axis=0, concat_axis=0, tiled=True).reshape(ny, nx)
    plane, xt, member, levels = lax.optimization_barrier((plane, xt, member, levels))
    right = lax.ppermute(plane, "col", [(i + 1, i) for i in range(cols - 1)])

    left = lax.ppermute(plane, "col", [(i, i + 1) for i in range(cols - 1)])
    b, own_rows_sum = call(
        own_kernel,
        "own",
        (((WIDTHS, tall, ny), F32), ((32, 128), F32)),
        (plane, xt, levels),
        scratch=(pltpu.VMEM((tall, ny), BF16), pltpu.VMEM((WIDTHS, tall, ny), F32)),
        flops=750_000_000,
        moved=7_000_000,
        special=100_000,
    )
    (part,) = call(
        cross_kernel,
        "cross",
        (((rows, 1, 128), F32),),
        (right, xt, levels, b, own_rows_sum),
        scratch=(pltpu.VMEM((32, 128), F32),),
        flops=250_000_000,
        moved=5_000_000,
        special=100_000,
    )
    part = lax.all_to_all(part, "row", split_axis=0, concat_axis=0, tiled=True)
    (part,) = call(gather_kernel, "regroup", (((cols, 1, 128), F32),), (part,))
    part = lax.all_to_all(part, "col", split_axis=0, concat_axis=0, tiled=True)

    (a,) = call(
        along_kernel,
        "along",
        (((WIDTHS, tall, ny), BF16),),
        (left, plane, right, xt, levels),
        scratch=(pltpu.VMEM((3 * HALF, ny), BF16),),
        flops=800_000_000,
        moved=4_000_000,
        special=300_000,
    )
    compliance, sensitivity = call(
        lambda *refs: combine_kernel(cells, *refs),
        "combine",
        (((CHANNELS,), F32), ((ny, nx), F32)),
        (part, member, a, plane, xt, levels),
        scratch=(pltpu.VMEM((VARIANTS, HALF, ny), F32),),
        flops=500_000_000,
        moved=5_000_000,
    )
    sensitivity = lax.all_to_all(
        sensitivity.reshape(planes, own_rows, nx), "row", split_axis=0, concat_axis=0, tiled=True
    )
    return compliance, sensitivity


def solution(mesh):
    in_specs = (P(None, "row", "col"), P(), P(), P())
    out_specs = (P(), P(None, "row", "col"))
    return jax.shard_map(
        per_device, mesh=mesh, in_specs=in_specs, out_specs=out_specs, check_vma=False
    )
```

```python
import jax
import jax.numpy as jnp
from jax import lax
from jax.experimental import pallas as pl
from jax.experimental.pallas import tpu as pltpu
from jax.sharding import PartitionSpec as P

VARIANTS = 3
WIDTHS = 10
CHANNELS = 30
HALF = 128
SHARPNESS = 8.0
SPREAD_FLOOR = 0.0001

F32 = jnp.float32
BF16 = jnp.bfloat16
VMEM = pl.BlockSpec(memory_space=pltpu.VMEM)
SMEM = pl.BlockSpec(memory_space=pltpu.SMEM)
MIB = 1024 * 1024


def bands_kernel(sigma_ref, width_ref, index_ref, xt_ref, member_ref, level_ref):
    row = lax.broadcasted_iota(jnp.int32, (HALF, HALF), 0)
    col = lax.broadcasted_iota(jnp.int32, (HALF, HALF), 1)
    gap = col - row
    gap_f = gap.astype(F32)
    squares = ((gap_f - HALF) ** 2, gap_f * gap_f, (gap_f + HALF) ** 2)
    masks = (gap >= 0, None, gap <= 0)
    taps = lax.broadcasted_iota(jnp.int32, (1, HALF), 1).astype(F32) + 1.0
    for w in range(WIDTHS):
        sigma = jnp.full((1, HALF), sigma_ref[w], F32)
        scale = -1.0 / (2.0 * sigma * sigma)
        total = 1.0 + 2.0 * jnp.sum(jnp.exp(taps * taps * scale), axis=1, keepdims=True)
        inverse = 1.0 / total
        blocks = []
        for square, mask in zip(squares, masks):
            value = jnp.exp(square * scale) * inverse
            if mask is not None:
                value = jnp.where(mask, value, 0.0)
            blocks.append(value.astype(BF16))
        before, middle, after = blocks
        rows = slice(w * HALF, (w + 1) * HALF)
        xt_ref[rows, 0:HALF] = before
        xt_ref[rows, HALF : 2 * HALF] = middle
        xt_ref[rows, 2 * HALF : 3 * HALF] = after
    lane = lax.broadcasted_iota(jnp.int32, (1, 128), 1)
    for c in range(CHANNELS):
        pair = (c // WIDTHS) * WIDTHS + width_ref[c]
        member_ref[c : c + 1, :] = (lane == pair).astype(F32)
    member_ref[CHANNELS:32, :] = jnp.zeros((32 - CHANNELS, 128), F32)
    for v in range(VARIANTS):
        level = jnp.full((1, 128), index_ref[v].astype(F32) * (1.0 / 16.0), F32)
        low = jnp.tanh(SHARPNESS * level)
        high = jnp.tanh(SHARPNESS * (1.0 - level))
        level_ref[v : v + 1, :] = level
        level_ref[8 + v : 9 + v, :] = low
        level_ref[16 + v : 17 + v, :] = 1.0 / (low + high)


def column_to_row(column):
    rows = column.shape[0]
    at = lax.broadcasted_iota(jnp.int32, (rows, 128), 0) == lax.broadcasted_iota(jnp.int32, (rows, 128), 1)
    return jnp.sum(jnp.where(at, jnp.broadcast_to(column, (rows, 128)), 0.0), axis=0, keepdims=True)


def constants(level_ref, v, width):
    rows = [level_ref[8 * i + v : 8 * i + v + 1, :] for i in range(3)]
    return [jnp.concatenate([row] * (width // 128), axis=1) for row in rows]


def project(side, level, low, inverse):
    inner = jnp.tanh(SHARPNESS * (side - level))
    return ((low + inner) * inverse).astype(BF16), inner


def square_band(xt_ref, w):
    rows = pl.ds(w * HALF, HALF)
    return jnp.concatenate([xt_ref[rows, HALF : 3 * HALF], xt_ref[rows, 0 : 2 * HALF]], axis=0)


def own_kernel(own_ref, xt_ref, level_ref, b_ref, rows_ref, p_ref, a_ref):
    ny = own_ref.shape[0]
    own = own_ref[...].T
    for v in range(VARIANTS):
        level, low, inverse = constants(level_ref, v, ny)
        value, _ = project(own, level, low, inverse)
        p_ref[v * HALF : (v + 1) * HALF, :] = value
    rows_ref[...] = jnp.zeros_like(rows_ref)
    for v in range(VARIANTS):
        part = p_ref[v * HALF : (v + 1) * HALF, :]
        along = jnp.dot(xt_ref[:, HALF : 2 * HALF], part, preferred_element_type=F32)
        a_ref[:, v * HALF : (v + 1) * HALF, :] = along.reshape(WIDTHS, HALF, ny)
    for w in range(WIDTHS):
        b = jnp.dot(p_ref[...], square_band(xt_ref, w), preferred_element_type=F32)
        b_ref[w] = b
        product = a_ref[w] * b
        for v in range(VARIANTS):
            line = jnp.sum(product[v * HALF : (v + 1) * HALF, :], axis=0, keepdims=True)
            rows_ref[v * WIDTHS + w : v * WIDTHS + w + 1, :] = line[:, 0:128] + line[:, 128:256]


def cross_kernel(right_ref, xt_ref, level_ref, b_ref, own_rows_ref, part_ref, rows_ref):
    ny = right_ref.shape[0]
    right = right_ref[...].T
    rows_ref[...] = own_rows_ref[...]
    for v in range(VARIANTS):
        level, low, inverse = constants(level_ref, v, ny)
        value, _ = project(right, level, low, inverse)
        along = jnp.dot(xt_ref[:, 2 * HALF : 3 * HALF], value, preferred_element_type=F32)
        for w in range(WIDTHS):
            product = along[w * HALF : (w + 1) * HALF, :] * b_ref[w, v * HALF : (v + 1) * HALF, :]
            line = jnp.sum(product, axis=0, keepdims=True)
            k = v * WIDTHS + w
            rows_ref[k : k + 1, :] += 2.0 * (line[:, 0:128] + line[:, 128:256])
    sums = column_to_row(jnp.sum(rows_ref[...], axis=1, keepdims=True))
    part_ref[...] = jnp.broadcast_to(sums.reshape(1, 1, 128), part_ref.shape)


def along_kernel(left_ref, own_ref, right_ref, xt_ref, level_ref, a_ref, p_ref):
    ny = left_ref.shape[0]
    left, own, right = left_ref[...].T, own_ref[...].T, right_ref[...].T
    for v in range(VARIANTS):
        level, low, inverse = constants(level_ref, v, ny)
        p_ref[0:HALF, :] = project(left, level, low, inverse)[0]
        p_ref[HALF : 2 * HALF, :] = project(own, level, low, inverse)[0]
        p_ref[2 * HALF : 3 * HALF, :] = project(right, level, low, inverse)[0]
        along = jnp.dot(xt_ref[...], p_ref[...], preferred_element_type=F32).astype(BF16)
        a_ref[:, v * HALF : (v + 1) * HALF, :] = along.reshape(WIDTHS, HALF, ny)


def gather_kernel(in_ref, out_ref):
    total = jnp.sum(in_ref[...], axis=0, keepdims=True)
    out_ref[...] = jnp.broadcast_to(total, out_ref.shape)


def combine_kernel(cells, sums_ref, member_ref, a_ref, own_ref, xt_ref, level_ref, compliance_ref, out_ref, total_ref):
    pairs = jnp.sum(sums_ref[...], axis=0) * (1.0 / cells)
    member = member_ref[...]
    compliance = jnp.sum(member * pairs, axis=1, keepdims=True)
    valid = lax.broadcasted_iota(jnp.int32, (32, 1), 0) < CHANNELS
    mean = jnp.sum(compliance, axis=0, keepdims=True) * (1.0 / CHANNELS)
    away = jnp.where(valid, compliance - mean, 0.0)
    spread = jnp.sqrt(jnp.sum(away * away, axis=0, keepdims=True) * (1.0 / CHANNELS) + SPREAD_FLOOR)
    weight = (1.0 + away / spread) * (2.0 / CHANNELS)
    per_pair = jnp.sum(member * weight, axis=0, keepdims=True)
    compliance_ref[...] = column_to_row(compliance)[0, :CHANNELS]
    for w in range(WIDTHS):
        field = jnp.dot(a_ref[w], square_band(xt_ref, w), preferred_element_type=F32)
        for v in range(VARIANTS):
            k = v * WIDTHS + w
            term = per_pair[:, k : k + 1] * field[v * HALF : (v + 1) * HALF, :]
            total_ref[v] = term if w == 0 else total_ref[v] + term
    own = own_ref[...].T
    total = None
    for v in range(VARIANTS):
        level, low, inverse = constants(level_ref, v, own.shape[1])
        inner = jnp.tanh(SHARPNESS * (own - level))
        term = total_ref[v] * (SHARPNESS * (1.0 - inner * inner) * inverse)
        total = term if total is None else total + term
    out_ref[...] = total.T


def call(kernel, name, out, inputs, scratch=(), specs=None, flops=0, moved=0, special=0):
    return pl.pallas_call(
        kernel,
        out_shape=tuple(jax.ShapeDtypeStruct(shape, dtype) for shape, dtype in out),
        in_specs=specs or [VMEM] * len(inputs),
        out_specs=(VMEM,) * len(out),
        scratch_shapes=list(scratch),
        compiler_params=pltpu.CompilerParams(vmem_limit_bytes=24 * MIB),
        cost_estimate=pl.CostEstimate(flops=flops, bytes_accessed=moved, transcendentals=special),
        name=name,
    )(*inputs)


def per_device(density, threshold_index, channel_width, sigma_table):
    planes, own_rows, nx = density.shape
    rows, cols = lax.axis_size("row"), lax.axis_size("col")
    ny = own_rows * rows
    cells = float(planes * ny * nx * cols)
    tall = VARIANTS * HALF

    xt, member, levels = call(
        bands_kernel,
        "bands",
        (((WIDTHS * HALF, 3 * HALF), BF16), ((32, 128), F32), ((24, 128), F32)),
        (sigma_table, channel_width, threshold_index),
        specs=[SMEM] * 3,
        flops=10_000_000,
        moved=2_500_000,
        special=500_000,
    )
    plane = lax.all_to_all(density, "row", split_axis=0, concat_axis=0, tiled=True).reshape(ny, nx)
    plane, xt, member, levels = lax.optimization_barrier((plane, xt, member, levels))
    right = lax.ppermute(plane, "col", [(i + 1, i) for i in range(cols - 1)])

    left = lax.ppermute(plane, "col", [(i, i + 1) for i in range(cols - 1)])
    b, own_rows_sum = call(
        own_kernel,
        "own",
        (((WIDTHS, tall, ny), F32), ((32, 128), F32)),
        (plane, xt, levels),
        scratch=(pltpu.VMEM((tall, ny), BF16), pltpu.VMEM((WIDTHS, tall, ny), F32)),
        flops=750_000_000,
        moved=7_000_000,
        special=100_000,
    )
    (part,) = call(
        cross_kernel,
        "cross",
        (((cols, 1, 128), F32),),
        (right, xt, levels, b, own_rows_sum),
        scratch=(pltpu.VMEM((32, 128), F32),),
        flops=250_000_000,
        moved=5_000_000,
        special=100_000,
    )
    part = lax.all_to_all(part, "col", split_axis=0, concat_axis=0, tiled=True)
    (a,) = call(
        along_kernel,
        "along",
        (((WIDTHS, tall, ny), BF16),),
        (left, plane, right, xt, levels),
        scratch=(pltpu.VMEM((3 * HALF, ny), BF16),),
        flops=800_000_000,
        moved=4_000_000,
        special=300_000,
    )
    part, a = lax.optimization_barrier((part, a))
    (part,) = call(gather_kernel, "regroup", (((rows, 1, 128), F32),), (part,))
    part = lax.all_to_all(part, "row", split_axis=0, concat_axis=0, tiled=True)

    compliance, sensitivity = call(
        lambda *refs: combine_kernel(cells, *refs),
        "combine",
        (((CHANNELS,), F32), ((ny, nx), F32)),
        (part, member, a, plane, xt, levels),
        scratch=(pltpu.VMEM((VARIANTS, HALF, ny), F32),),
        flops=500_000_000,
        moved=5_000_000,
    )
    sensitivity = lax.all_to_all(
        sensitivity.reshape(planes, own_rows, nx), "row", split_axis=0, concat_axis=0, tiled=True
    )
    return compliance, sensitivity


def solution(mesh):
    in_specs = (P(None, "row", "col"), P(), P(), P())
    out_specs = (P(), P(None, "row", "col"))
    return jax.shard_map(
        per_device, mesh=mesh, in_specs=in_specs, out_specs=out_specs, check_vma=False
    )
```

```python
from functools import partial

import jax
import jax.numpy as jnp
from jax import lax
from jax.experimental import pallas as pl
from jax.experimental.pallas import tpu as pltpu
from jax.sharding import PartitionSpec as P

VARIANTS = 3
WIDTHS = 10
CHANNELS = 30
HALF = 128
SHARPNESS = 8.0
SPREAD_FLOOR = 0.0001

F32 = jnp.float32
BF16 = jnp.bfloat16
VMEM = pl.BlockSpec(memory_space=pltpu.VMEM)
SMEM = pl.BlockSpec(memory_space=pltpu.SMEM)
MIB = 1024 * 1024
FIRST = {"row": 18, "col": 8}


def bands_kernel(sigma_ref, width_ref, index_ref, xt_ref, member_ref, level_ref):
    row = lax.broadcasted_iota(jnp.int32, (HALF, HALF), 0)
    col = lax.broadcasted_iota(jnp.int32, (HALF, HALF), 1)
    gap = col - row
    gap_f = gap.astype(F32)
    squares = ((gap_f - HALF) ** 2, gap_f * gap_f, (gap_f + HALF) ** 2)
    masks = (gap >= 0, None, gap <= 0)
    taps = lax.broadcasted_iota(jnp.int32, (1, HALF), 1).astype(F32) + 1.0
    for w in range(WIDTHS):
        sigma = jnp.full((1, HALF), sigma_ref[w], F32)
        scale = -1.0 / (2.0 * sigma * sigma)
        total = 1.0 + 2.0 * jnp.sum(jnp.exp(taps * taps * scale), axis=1, keepdims=True)
        inverse = 1.0 / total
        blocks = []
        for square, mask in zip(squares, masks):
            value = jnp.exp(square * scale) * inverse
            if mask is not None:
                value = jnp.where(mask, value, 0.0)
            blocks.append(value.astype(BF16))
        before, middle, after = blocks
        rows = slice(w * HALF, (w + 1) * HALF)
        xt_ref[rows, 0:HALF] = before
        xt_ref[rows, HALF : 2 * HALF] = middle
        xt_ref[rows, 2 * HALF : 3 * HALF] = after
    lane = lax.broadcasted_iota(jnp.int32, (1, 128), 1)
    for c in range(CHANNELS):
        pair = (c // WIDTHS) * WIDTHS + width_ref[c]
        member_ref[c : c + 1, :] = (lane == pair).astype(F32)
    member_ref[CHANNELS:32, :] = jnp.zeros((32 - CHANNELS, 128), F32)
    for v in range(VARIANTS):
        level = jnp.full((1, 128), index_ref[v].astype(F32) * (1.0 / 16.0), F32)
        low = jnp.tanh(SHARPNESS * level)
        high = jnp.tanh(SHARPNESS * (1.0 - level))
        level_ref[v : v + 1, :] = level
        level_ref[8 + v : 9 + v, :] = low
        level_ref[16 + v : 17 + v, :] = 1.0 / (low + high)


def regroup(x, axis):
    size = lax.axis_size(axis)
    order = [(FIRST[axis] + i) % size for i in range(size)]
    return lax.all_to_all(x, axis, split_axis=0, concat_axis=0, axis_index_groups=[order], tiled=True)


def turned(x, rows):
    rows %= x.shape[0]
    return x if rows == 0 else jnp.concatenate([x[-rows:], x[:-rows]], axis=0)


def columns(plane_ref, turn):
    return turned(plane_ref[...], turn).T


def column_to_row(column):
    rows = column.shape[0]
    at = lax.broadcasted_iota(jnp.int32, (rows, 128), 0) == lax.broadcasted_iota(jnp.int32, (rows, 128), 1)
    return jnp.sum(jnp.where(at, jnp.broadcast_to(column, (rows, 128)), 0.0), axis=0, keepdims=True)


def constants(level_ref, v, width):
    rows = [level_ref[8 * i + v : 8 * i + v + 1, :] for i in range(3)]
    return [jnp.concatenate([row] * (width // 128), axis=1) for row in rows]


def project(side, level, low, inverse):
    inner = jnp.tanh(SHARPNESS * (side - level))
    return ((low + inner) * inverse).astype(BF16), inner


def square_band(xt_ref, w):
    rows = pl.ds(w * HALF, HALF)
    return jnp.concatenate([xt_ref[rows, HALF : 3 * HALF], xt_ref[rows, 0 : 2 * HALF]], axis=0)


def own_kernel(turn, own_ref, xt_ref, level_ref, b_ref, rows_ref, p_ref, a_ref):
    ny = own_ref.shape[0]
    own = columns(own_ref, turn)
    for v in range(VARIANTS):
        level, low, inverse = constants(level_ref, v, ny)
        value, _ = project(own, level, low, inverse)
        p_ref[v * HALF : (v + 1) * HALF, :] = value
    rows_ref[...] = jnp.zeros_like(rows_ref)
    for v in range(VARIANTS):
        part = p_ref[v * HALF : (v + 1) * HALF, :]
        along = jnp.dot(xt_ref[:, HALF : 2 * HALF], part, preferred_element_type=F32)
        a_ref[:, v * HALF : (v + 1) * HALF, :] = along.reshape(WIDTHS, HALF, ny)
    for w in range(WIDTHS):
        b = jnp.dot(p_ref[...], square_band(xt_ref, w), preferred_element_type=F32)
        b_ref[w] = b
        product = a_ref[w] * b
        for v in range(VARIANTS):
            line = jnp.sum(product[v * HALF : (v + 1) * HALF, :], axis=0, keepdims=True)
            rows_ref[v * WIDTHS + w : v * WIDTHS + w + 1, :] = line[:, 0:128] + line[:, 128:256]


def cross_kernel(turn, right_ref, xt_ref, level_ref, b_ref, own_rows_ref, part_ref, rows_ref):
    ny = right_ref.shape[0]
    right = columns(right_ref, turn)
    rows_ref[...] = own_rows_ref[...]
    for v in range(VARIANTS):
        level, low, inverse = constants(level_ref, v, ny)
        value, _ = project(right, level, low, inverse)
        along = jnp.dot(xt_ref[:, 2 * HALF : 3 * HALF], value, preferred_element_type=F32)
        for w in range(WIDTHS):
            product = along[w * HALF : (w + 1) * HALF, :] * b_ref[w, v * HALF : (v + 1) * HALF, :]
            line = jnp.sum(product, axis=0, keepdims=True)
            k = v * WIDTHS + w
            rows_ref[k : k + 1, :] += 2.0 * (line[:, 0:128] + line[:, 128:256])
    sums = column_to_row(jnp.sum(rows_ref[...], axis=1, keepdims=True))
    part_ref[...] = jnp.broadcast_to(sums.reshape(1, 1, 128), part_ref.shape)


def along_kernel(turn, left_ref, own_ref, right_ref, xt_ref, level_ref, a_ref, p_ref):
    ny = left_ref.shape[0]
    left, own, right = [columns(ref, turn) for ref in (left_ref, own_ref, right_ref)]
    for v in range(VARIANTS):
        level, low, inverse = constants(level_ref, v, ny)
        p_ref[0:HALF, :] = project(left, level, low, inverse)[0]
        p_ref[HALF : 2 * HALF, :] = project(own, level, low, inverse)[0]
        p_ref[2 * HALF : 3 * HALF, :] = project(right, level, low, inverse)[0]
        along = jnp.dot(xt_ref[...], p_ref[...], preferred_element_type=F32).astype(BF16)
        a_ref[:, v * HALF : (v + 1) * HALF, :] = along.reshape(WIDTHS, HALF, ny)


def gather_kernel(in_ref, out_ref):
    total = jnp.sum(in_ref[...], axis=0, keepdims=True)
    out_ref[...] = jnp.broadcast_to(total, out_ref.shape)


def combine_kernel(cells, turn, sums_ref, member_ref, a_ref, own_ref, xt_ref, level_ref, compliance_ref, out_ref, total_ref):
    pairs = jnp.sum(sums_ref[...], axis=0) * (1.0 / cells)
    member = member_ref[...]
    compliance = jnp.sum(member * pairs, axis=1, keepdims=True)
    valid = lax.broadcasted_iota(jnp.int32, (32, 1), 0) < CHANNELS
    mean = jnp.sum(compliance, axis=0, keepdims=True) * (1.0 / CHANNELS)
    away = jnp.where(valid, compliance - mean, 0.0)
    spread = jnp.sqrt(jnp.sum(away * away, axis=0, keepdims=True) * (1.0 / CHANNELS) + SPREAD_FLOOR)
    weight = (1.0 + away / spread) * (2.0 / CHANNELS)
    per_pair = jnp.sum(member * weight, axis=0, keepdims=True)
    compliance_ref[...] = column_to_row(compliance)[0, :CHANNELS]
    for w in range(WIDTHS):
        field = jnp.dot(a_ref[w], square_band(xt_ref, w), preferred_element_type=F32)
        for v in range(VARIANTS):
            k = v * WIDTHS + w
            term = per_pair[:, k : k + 1] * field[v * HALF : (v + 1) * HALF, :]
            total_ref[v] = term if w == 0 else total_ref[v] + term
    own = columns(own_ref, turn)
    total = None
    for v in range(VARIANTS):
        level, low, inverse = constants(level_ref, v, own.shape[1])
        inner = jnp.tanh(SHARPNESS * (own - level))
        term = total_ref[v] * (SHARPNESS * (1.0 - inner * inner) * inverse)
        total = term if total is None else total + term
    out_ref[...] = turned(total.T, -turn)


def call(kernel, name, out, inputs, scratch=(), specs=None, flops=0, moved=0, special=0):
    return pl.pallas_call(
        kernel,
        out_shape=tuple(jax.ShapeDtypeStruct(shape, dtype) for shape, dtype in out),
        in_specs=specs or [VMEM] * len(inputs),
        out_specs=(VMEM,) * len(out),
        scratch_shapes=list(scratch),
        compiler_params=pltpu.CompilerParams(vmem_limit_bytes=24 * MIB),
        cost_estimate=pl.CostEstimate(flops=flops, bytes_accessed=moved, transcendentals=special),
        name=name,
    )(*inputs)


def per_device(density, threshold_index, channel_width, sigma_table):
    planes, own_rows, nx = density.shape
    rows, cols = lax.axis_size("row"), lax.axis_size("col")
    ny = own_rows * rows
    cells = float(planes * ny * nx * cols)
    tall = VARIANTS * HALF
    turn = FIRST["row"] * own_rows

    xt, member, levels = call(
        bands_kernel,
        "bands",
        (((WIDTHS * HALF, 3 * HALF), BF16), ((32, 128), F32), ((24, 128), F32)),
        (sigma_table, channel_width, threshold_index),
        specs=[SMEM] * 3,
        flops=10_000_000,
        moved=2_500_000,
        special=500_000,
    )
    plane = regroup(density, "row").reshape(ny, nx)
    plane, xt, member, levels = lax.optimization_barrier((plane, xt, member, levels))
    right = lax.ppermute(plane, "col", [(i + 1, i) for i in range(cols - 1)])

    left = lax.ppermute(plane, "col", [(i, i + 1) for i in range(cols - 1)])
    b, own_rows_sum = call(
        partial(own_kernel, turn),
        "own",
        (((WIDTHS, tall, ny), F32), ((32, 128), F32)),
        (plane, xt, levels),
        scratch=(pltpu.VMEM((tall, ny), BF16), pltpu.VMEM((WIDTHS, tall, ny), F32)),
        flops=750_000_000,
        moved=7_000_000,
        special=100_000,
    )
    (part,) = call(
        partial(cross_kernel, turn),
        "cross",
        (((cols, 1, 128), F32),),
        (right, xt, levels, b, own_rows_sum),
        scratch=(pltpu.VMEM((32, 128), F32),),
        flops=250_000_000,
        moved=5_000_000,
        special=100_000,
    )
    part = regroup(part, "col")
    (a,) = call(
        partial(along_kernel, turn),
        "along",
        (((WIDTHS, tall, ny), BF16),),
        (left, plane, right, xt, levels),
        scratch=(pltpu.VMEM((3 * HALF, ny), BF16),),
        flops=800_000_000,
        moved=4_000_000,
        special=300_000,
    )
    part, a = lax.optimization_barrier((part, a))
    (part,) = call(gather_kernel, "regroup", (((rows, 1, 128), F32),), (part,))
    part = regroup(part, "row")

    compliance, sensitivity = call(
        partial(combine_kernel, cells, turn),
        "combine",
        (((CHANNELS,), F32), ((ny, nx), F32)),
        (part, member, a, plane, xt, levels),
        scratch=(pltpu.VMEM((VARIANTS, HALF, ny), F32),),
        flops=500_000_000,
        moved=5_000_000,
    )
    sensitivity = regroup(sensitivity.reshape(planes, own_rows, nx), "row")
    return compliance, sensitivity


def solution(mesh):
    in_specs = (P(None, "row", "col"), P(), P(), P())
    out_specs = (P(), P(None, "row", "col"))
    return jax.shard_map(
        per_device, mesh=mesh, in_specs=in_specs, out_specs=out_specs, check_vma=False
    )
```

```python
from functools import partial

import jax
import jax.numpy as jnp
from jax import lax
from jax.experimental import pallas as pl
from jax.experimental.pallas import tpu as pltpu
from jax.sharding import PartitionSpec as P

VARIANTS = 3
WIDTHS = 10
CHANNELS = 30
HALF = 128
SHARPNESS = 8.0
SPREAD_FLOOR = 0.0001

F32 = jnp.float32
BF16 = jnp.bfloat16
VMEM = pl.BlockSpec(memory_space=pltpu.VMEM)
SMEM = pl.BlockSpec(memory_space=pltpu.SMEM)
MIB = 1024 * 1024
FIRST = {"row": 22, "col": 9}


def bands_kernel(sigma_ref, width_ref, index_ref, xt_ref, member_ref, level_ref):
    row = lax.broadcasted_iota(jnp.int32, (HALF, HALF), 0)
    col = lax.broadcasted_iota(jnp.int32, (HALF, HALF), 1)
    gap = col - row
    gap_f = gap.astype(F32)
    squares = ((gap_f - HALF) ** 2, gap_f * gap_f, (gap_f + HALF) ** 2)
    masks = (gap >= 0, None, gap <= 0)
    taps = lax.broadcasted_iota(jnp.int32, (1, HALF), 1).astype(F32) + 1.0
    for w in range(WIDTHS):
        sigma = jnp.full((1, HALF), sigma_ref[w], F32)
        scale = -1.0 / (2.0 * sigma * sigma)
        total = 1.0 + 2.0 * jnp.sum(jnp.exp(taps * taps * scale), axis=1, keepdims=True)
        inverse = 1.0 / total
        blocks = []
        for square, mask in zip(squares, masks):
            value = jnp.exp(square * scale) * inverse
            if mask is not None:
                value = jnp.where(mask, value, 0.0)
            blocks.append(value.astype(BF16))
        before, middle, after = blocks
        rows = slice(w * HALF, (w + 1) * HALF)
        xt_ref[rows, 0:HALF] = before
        xt_ref[rows, HALF : 2 * HALF] = middle
        xt_ref[rows, 2 * HALF : 3 * HALF] = after
    lane = lax.broadcasted_iota(jnp.int32, (1, 128), 1)
    for c in range(CHANNELS):
        pair = (c // WIDTHS) * WIDTHS + width_ref[c]
        member_ref[c : c + 1, :] = (lane == pair).astype(F32)
    member_ref[CHANNELS:32, :] = jnp.zeros((32 - CHANNELS, 128), F32)
    for v in range(VARIANTS):
        level = jnp.full((1, 128), index_ref[v].astype(F32) * (1.0 / 16.0), F32)
        low = jnp.tanh(SHARPNESS * level)
        high = jnp.tanh(SHARPNESS * (1.0 - level))
        level_ref[v : v + 1, :] = level
        level_ref[8 + v : 9 + v, :] = low
        level_ref[16 + v : 17 + v, :] = 1.0 / (low + high)


def regroup(x, axis):
    size = lax.axis_size(axis)
    order = [(FIRST[axis] + i) % size for i in range(size)]
    return lax.all_to_all(x, axis, split_axis=0, concat_axis=0, axis_index_groups=[order], tiled=True)


def turned(x, rows):
    rows %= x.shape[0]
    return x if rows == 0 else jnp.concatenate([x[-rows:], x[:-rows]], axis=0)


def columns(plane_ref, turn):
    return turned(plane_ref[...], turn).T


def column_to_row(column):
    rows = column.shape[0]
    at = lax.broadcasted_iota(jnp.int32, (rows, 128), 0) == lax.broadcasted_iota(jnp.int32, (rows, 128), 1)
    return jnp.sum(jnp.where(at, jnp.broadcast_to(column, (rows, 128)), 0.0), axis=0, keepdims=True)


def constants(level_ref, v, width):
    rows = [level_ref[8 * i + v : 8 * i + v + 1, :] for i in range(3)]
    return [jnp.concatenate([row] * (width // 128), axis=1) for row in rows]


def project(side, level, low, inverse):
    inner = jnp.tanh(SHARPNESS * (side - level))
    return ((low + inner) * inverse).astype(BF16), inner


def square_band(xt_ref, w):
    rows = pl.ds(w * HALF, HALF)
    return jnp.concatenate([xt_ref[rows, HALF : 3 * HALF], xt_ref[rows, 0 : 2 * HALF]], axis=0)


def own_kernel(turn, own_ref, xt_ref, level_ref, b_ref, rows_ref, p_ref, a_ref):
    ny = own_ref.shape[0]
    own = columns(own_ref, turn)
    for v in range(VARIANTS):
        level, low, inverse = constants(level_ref, v, ny)
        value, _ = project(own, level, low, inverse)
        p_ref[v * HALF : (v + 1) * HALF, :] = value
    rows_ref[...] = jnp.zeros_like(rows_ref)
    for v in range(VARIANTS):
        part = p_ref[v * HALF : (v + 1) * HALF, :]
        along = jnp.dot(xt_ref[:, HALF : 2 * HALF], part, preferred_element_type=F32)
        a_ref[:, v * HALF : (v + 1) * HALF, :] = along.reshape(WIDTHS, HALF, ny)
    for w in range(WIDTHS):
        b = jnp.dot(p_ref[...], square_band(xt_ref, w), preferred_element_type=F32)
        b_ref[w] = b
        product = a_ref[w] * b
        for v in range(VARIANTS):
            line = jnp.sum(product[v * HALF : (v + 1) * HALF, :], axis=0, keepdims=True)
            rows_ref[v * WIDTHS + w : v * WIDTHS + w + 1, :] = line[:, 0:128] + line[:, 128:256]


def cross_kernel(turn, right_ref, xt_ref, level_ref, b_ref, own_rows_ref, part_ref, rows_ref):
    ny = right_ref.shape[0]
    right = columns(right_ref, turn)
    rows_ref[...] = own_rows_ref[...]
    for v in range(VARIANTS):
        level, low, inverse = constants(level_ref, v, ny)
        value, _ = project(right, level, low, inverse)
        along = jnp.dot(xt_ref[:, 2 * HALF : 3 * HALF], value, preferred_element_type=F32)
        for w in range(WIDTHS):
            product = along[w * HALF : (w + 1) * HALF, :] * b_ref[w, v * HALF : (v + 1) * HALF, :]
            line = jnp.sum(product, axis=0, keepdims=True)
            k = v * WIDTHS + w
            rows_ref[k : k + 1, :] += 2.0 * (line[:, 0:128] + line[:, 128:256])
    sums = column_to_row(jnp.sum(rows_ref[...], axis=1, keepdims=True))
    part_ref[...] = jnp.broadcast_to(sums.reshape(1, 1, 128), part_ref.shape)


def along_kernel(turn, left_ref, own_ref, right_ref, xt_ref, level_ref, a_ref, p_ref):
    ny = left_ref.shape[0]
    left, own, right = [columns(ref, turn) for ref in (left_ref, own_ref, right_ref)]
    for v in range(VARIANTS):
        level, low, inverse = constants(level_ref, v, ny)
        p_ref[0:HALF, :] = project(left, level, low, inverse)[0]
        p_ref[HALF : 2 * HALF, :] = project(own, level, low, inverse)[0]
        p_ref[2 * HALF : 3 * HALF, :] = project(right, level, low, inverse)[0]
        along = jnp.dot(xt_ref[...], p_ref[...], preferred_element_type=F32).astype(BF16)
        a_ref[:, v * HALF : (v + 1) * HALF, :] = along.reshape(WIDTHS, HALF, ny)


def gather_kernel(in_ref, out_ref):
    total = jnp.sum(in_ref[...], axis=0, keepdims=True)
    out_ref[...] = jnp.broadcast_to(total, out_ref.shape)


def combine_kernel(cells, turn, sums_ref, member_ref, a_ref, own_ref, xt_ref, level_ref, compliance_ref, out_ref, total_ref):
    pairs = jnp.sum(sums_ref[...], axis=0) * (1.0 / cells)
    member = member_ref[...]
    compliance = jnp.sum(member * pairs, axis=1, keepdims=True)
    valid = lax.broadcasted_iota(jnp.int32, (32, 1), 0) < CHANNELS
    mean = jnp.sum(compliance, axis=0, keepdims=True) * (1.0 / CHANNELS)
    away = jnp.where(valid, compliance - mean, 0.0)
    spread = jnp.sqrt(jnp.sum(away * away, axis=0, keepdims=True) * (1.0 / CHANNELS) + SPREAD_FLOOR)
    weight = (1.0 + away / spread) * (2.0 / CHANNELS)
    per_pair = jnp.sum(member * weight, axis=0, keepdims=True)
    compliance_ref[...] = column_to_row(compliance)[0, :CHANNELS]
    for w in range(WIDTHS):
        field = jnp.dot(a_ref[w], square_band(xt_ref, w), preferred_element_type=F32)
        for v in range(VARIANTS):
            k = v * WIDTHS + w
            term = per_pair[:, k : k + 1] * field[v * HALF : (v + 1) * HALF, :]
            total_ref[v] = term if w == 0 else total_ref[v] + term
    own = columns(own_ref, turn)
    total = None
    for v in range(VARIANTS):
        level, low, inverse = constants(level_ref, v, own.shape[1])
        inner = jnp.tanh(SHARPNESS * (own - level))
        term = total_ref[v] * (SHARPNESS * (1.0 - inner * inner) * inverse)
        total = term if total is None else total + term
    out_ref[...] = turned(total.T, -turn)


def call(kernel, name, out, inputs, scratch=(), specs=None, flops=0, moved=0, special=0):
    return pl.pallas_call(
        kernel,
        out_shape=tuple(jax.ShapeDtypeStruct(shape, dtype) for shape, dtype in out),
        in_specs=specs or [VMEM] * len(inputs),
        out_specs=(VMEM,) * len(out),
        scratch_shapes=list(scratch),
        compiler_params=pltpu.CompilerParams(vmem_limit_bytes=24 * MIB),
        cost_estimate=pl.CostEstimate(flops=flops, bytes_accessed=moved, transcendentals=special),
        name=name,
    )(*inputs)


def per_device(density, threshold_index, channel_width, sigma_table):
    planes, own_rows, nx = density.shape
    rows, cols = lax.axis_size("row"), lax.axis_size("col")
    ny = own_rows * rows
    cells = float(planes * ny * nx * cols)
    tall = VARIANTS * HALF
    turn = FIRST["row"] * own_rows

    xt, member, levels = call(
        bands_kernel,
        "bands",
        (((WIDTHS * HALF, 3 * HALF), BF16), ((32, 128), F32), ((24, 128), F32)),
        (sigma_table, channel_width, threshold_index),
        specs=[SMEM] * 3,
        flops=10_000_000,
        moved=2_500_000,
        special=500_000,
    )
    plane = regroup(density, "row").reshape(ny, nx)
    plane, xt, member, levels = lax.optimization_barrier((plane, xt, member, levels))
    right = lax.ppermute(plane, "col", [(i + 1, i) for i in range(cols - 1)])

    left = lax.ppermute(plane, "col", [(i, i + 1) for i in range(cols - 1)])
    b, own_rows_sum = call(
        partial(own_kernel, turn),
        "own",
        (((WIDTHS, tall, ny), F32), ((32, 128), F32)),
        (plane, xt, levels),
        scratch=(pltpu.VMEM((tall, ny), BF16), pltpu.VMEM((WIDTHS, tall, ny), F32)),
        flops=750_000_000,
        moved=7_000_000,
        special=100_000,
    )
    (part,) = call(
        partial(cross_kernel, turn),
        "cross",
        (((rows, 1, 128), F32),),
        (right, xt, levels, b, own_rows_sum),
        scratch=(pltpu.VMEM((32, 128), F32),),
        flops=250_000_000,
        moved=5_000_000,
        special=100_000,
    )
    part = regroup(part, "row")
    (part,) = call(gather_kernel, "regroup", (((cols, 1, 128), F32),), (part,))
    part = regroup(part, "col")

    (a,) = call(
        partial(along_kernel, turn),
        "along",
        (((WIDTHS, tall, ny), BF16),),
        (left, plane, right, xt, levels),
        scratch=(pltpu.VMEM((3 * HALF, ny), BF16),),
        flops=800_000_000,
        moved=4_000_000,
        special=300_000,
    )
    compliance, sensitivity = call(
        partial(combine_kernel, cells, turn),
        "combine",
        (((CHANNELS,), F32), ((ny, nx), F32)),
        (part, member, a, plane, xt, levels),
        scratch=(pltpu.VMEM((VARIANTS, HALF, ny), F32),),
        flops=500_000_000,
        moved=5_000_000,
    )
    sensitivity = regroup(sensitivity.reshape(planes, own_rows, nx), "row")
    return compliance, sensitivity


def solution(mesh):
    in_specs = (P(None, "row", "col"), P(), P(), P())
    out_specs = (P(), P(None, "row", "col"))
    return jax.shard_map(
        per_device, mesh=mesh, in_specs=in_specs, out_specs=out_specs, check_vma=False
    )
```

```python
from functools import partial

import jax
import jax.numpy as jnp
from jax import lax
from jax.experimental import pallas as pl
from jax.experimental.pallas import tpu as pltpu
from jax.sharding import PartitionSpec as P

VARIANTS = 3
WIDTHS = 10
CHANNELS = 30
HALF = 128
SHARPNESS = 8.0
SPREAD_FLOOR = 0.0001

F32 = jnp.float32
BF16 = jnp.bfloat16
VMEM = pl.BlockSpec(memory_space=pltpu.VMEM)
SMEM = pl.BlockSpec(memory_space=pltpu.SMEM)
MIB = 1024 * 1024
SCALE = 1024.0
FIRST = {"row": 22, "col": 9}


def bands_kernel(sigma_ref, width_ref, index_ref, xt_ref, member_ref, level_ref):
    row = lax.broadcasted_iota(jnp.int32, (HALF, HALF), 0)
    col = lax.broadcasted_iota(jnp.int32, (HALF, HALF), 1)
    gap = col - row
    gap_f = gap.astype(F32)
    squares = ((gap_f - HALF) ** 2, gap_f * gap_f, (gap_f + HALF) ** 2)
    masks = (gap >= 0, None, gap <= 0)
    taps = lax.broadcasted_iota(jnp.int32, (1, HALF), 1).astype(F32) + 1.0
    for w in range(WIDTHS):
        sigma = jnp.full((1, HALF), sigma_ref[w], F32)
        scale = -1.0 / (2.0 * sigma * sigma)
        total = 1.0 + 2.0 * jnp.sum(jnp.exp(taps * taps * scale), axis=1, keepdims=True)
        inverse = 1.0 / total
        blocks = []
        for square, mask in zip(squares, masks):
            value = jnp.exp(square * scale) * inverse
            if mask is not None:
                value = jnp.where(mask, value, 0.0)
            blocks.append(value.astype(BF16))
        before, middle, after = blocks
        rows = slice(w * HALF, (w + 1) * HALF)
        xt_ref[rows, 0:HALF] = before
        xt_ref[rows, HALF : 2 * HALF] = middle
        xt_ref[rows, 2 * HALF : 3 * HALF] = after
    lane = lax.broadcasted_iota(jnp.int32, (1, 128), 1)
    for c in range(CHANNELS):
        pair = (c // WIDTHS) * WIDTHS + width_ref[c]
        member_ref[c : c + 1, :] = (lane == pair).astype(F32)
    member_ref[CHANNELS:32, :] = jnp.zeros((32 - CHANNELS, 128), F32)
    for v in range(VARIANTS):
        level = jnp.full((1, 128), index_ref[v].astype(F32) * (1.0 / 16.0), F32)
        low = jnp.tanh(SHARPNESS * level)
        high = jnp.tanh(SHARPNESS * (1.0 - level))
        level_ref[v : v + 1, :] = level
        level_ref[8 + v : 9 + v, :] = low
        level_ref[16 + v : 17 + v, :] = 1.0 / (low + high)


def regroup(x, axis):
    size = lax.axis_size(axis)
    order = [(FIRST[axis] + i) % size for i in range(size)]
    return lax.all_to_all(x, axis, split_axis=0, concat_axis=0, axis_index_groups=[order], tiled=True)


def turned(x, rows):
    rows %= x.shape[0]
    return x if rows == 0 else jnp.concatenate([x[-rows:], x[:-rows]], axis=0)


def columns(plane_ref, turn):
    return turned(plane_ref[...], turn).T


def encode(x):
    power = x * SCALE
    for _ in range(3):
        power = power * power
    return jnp.where(x < 0.0, -power, power).astype(BF16)


def decode(code):
    power = code.astype(F32)
    root = jnp.abs(power)
    for _ in range(3):
        root = jnp.sqrt(root)
    return jnp.where(power < 0.0, -root, root) * (1.0 / SCALE)


def column_to_row(column):
    rows = column.shape[0]
    at = lax.broadcasted_iota(jnp.int32, (rows, 128), 0) == lax.broadcasted_iota(jnp.int32, (rows, 128), 1)
    return jnp.sum(jnp.where(at, jnp.broadcast_to(column, (rows, 128)), 0.0), axis=0, keepdims=True)


def constants(level_ref, v, width):
    rows = [level_ref[8 * i + v : 8 * i + v + 1, :] for i in range(3)]
    return [jnp.concatenate([row] * (width // 128), axis=1) for row in rows]


def project(side, level, low, inverse):
    inner = jnp.tanh(SHARPNESS * (side - level))
    return ((low + inner) * inverse).astype(BF16), inner


def square_band(xt_ref, w):
    rows = pl.ds(w * HALF, HALF)
    return jnp.concatenate([xt_ref[rows, HALF : 3 * HALF], xt_ref[rows, 0 : 2 * HALF]], axis=0)


def own_kernel(turn, own_ref, xt_ref, level_ref, b_ref, rows_ref, p_ref, a_ref):
    ny = own_ref.shape[0]
    own = columns(own_ref, turn)
    for v in range(VARIANTS):
        level, low, inverse = constants(level_ref, v, ny)
        value, _ = project(own, level, low, inverse)
        p_ref[v * HALF : (v + 1) * HALF, :] = value
    rows_ref[...] = jnp.zeros_like(rows_ref)
    for v in range(VARIANTS):
        part = p_ref[v * HALF : (v + 1) * HALF, :]
        along = jnp.dot(xt_ref[:, HALF : 2 * HALF], part, preferred_element_type=F32)
        a_ref[:, v * HALF : (v + 1) * HALF, :] = along.reshape(WIDTHS, HALF, ny)
    for w in range(WIDTHS):
        b = jnp.dot(p_ref[...], square_band(xt_ref, w), preferred_element_type=F32)
        b_ref[w] = b
        product = a_ref[w] * b
        for v in range(VARIANTS):
            line = jnp.sum(product[v * HALF : (v + 1) * HALF, :], axis=0, keepdims=True)
            rows_ref[v * WIDTHS + w : v * WIDTHS + w + 1, :] = line[:, 0:128] + line[:, 128:256]


def cross_kernel(turn, right_ref, xt_ref, level_ref, b_ref, own_rows_ref, part_ref, rows_ref):
    ny = right_ref.shape[0]
    right = columns(right_ref, turn)
    rows_ref[...] = own_rows_ref[...]
    for v in range(VARIANTS):
        level, low, inverse = constants(level_ref, v, ny)
        value, _ = project(right, level, low, inverse)
        along = jnp.dot(xt_ref[:, 2 * HALF : 3 * HALF], value, preferred_element_type=F32)
        for w in range(WIDTHS):
            product = along[w * HALF : (w + 1) * HALF, :] * b_ref[w, v * HALF : (v + 1) * HALF, :]
            line = jnp.sum(product, axis=0, keepdims=True)
            k = v * WIDTHS + w
            rows_ref[k : k + 1, :] += 2.0 * (line[:, 0:128] + line[:, 128:256])
    sums = column_to_row(jnp.sum(rows_ref[...], axis=1, keepdims=True))
    part_ref[...] = jnp.broadcast_to(sums.reshape(1, 1, 128), part_ref.shape)


def along_kernel(turn, left_ref, own_ref, right_ref, xt_ref, level_ref, a_ref, p_ref):
    ny = left_ref.shape[0]
    left, own, right = [columns(ref, turn) for ref in (left_ref, own_ref, right_ref)]
    for v in range(VARIANTS):
        level, low, inverse = constants(level_ref, v, ny)
        p_ref[0:HALF, :] = project(left, level, low, inverse)[0]
        p_ref[HALF : 2 * HALF, :] = project(own, level, low, inverse)[0]
        p_ref[2 * HALF : 3 * HALF, :] = project(right, level, low, inverse)[0]
        along = jnp.dot(xt_ref[...], p_ref[...], preferred_element_type=F32).astype(BF16)
        a_ref[:, v * HALF : (v + 1) * HALF, :] = along.reshape(WIDTHS, HALF, ny)


def gather_kernel(in_ref, out_ref):
    total = jnp.sum(in_ref[...], axis=0, keepdims=True)
    out_ref[...] = jnp.broadcast_to(total, out_ref.shape)


def combine_kernel(cells, turn, sums_ref, member_ref, a_ref, own_ref, xt_ref, level_ref, compliance_ref, out_ref, total_ref):
    pairs = jnp.sum(sums_ref[...], axis=0) * (1.0 / cells)
    member = member_ref[...]
    compliance = jnp.sum(member * pairs, axis=1, keepdims=True)
    valid = lax.broadcasted_iota(jnp.int32, (32, 1), 0) < CHANNELS
    mean = jnp.sum(compliance, axis=0, keepdims=True) * (1.0 / CHANNELS)
    away = jnp.where(valid, compliance - mean, 0.0)
    spread = jnp.sqrt(jnp.sum(away * away, axis=0, keepdims=True) * (1.0 / CHANNELS) + SPREAD_FLOOR)
    weight = (1.0 + away / spread) * (2.0 / CHANNELS)
    per_pair = jnp.sum(member * weight, axis=0, keepdims=True)
    compliance_ref[...] = column_to_row(compliance)[0, :CHANNELS]
    for w in range(WIDTHS):
        field = jnp.dot(a_ref[w], square_band(xt_ref, w), preferred_element_type=F32)
        for v in range(VARIANTS):
            k = v * WIDTHS + w
            term = per_pair[:, k : k + 1] * field[v * HALF : (v + 1) * HALF, :]
            total_ref[v] = term if w == 0 else total_ref[v] + term
    own = columns(own_ref, turn)
    total = None
    for v in range(VARIANTS):
        level, low, inverse = constants(level_ref, v, own.shape[1])
        inner = jnp.tanh(SHARPNESS * (own - level))
        term = total_ref[v] * (SHARPNESS * (1.0 - inner * inner) * inverse)
        total = term if total is None else total + term
    out_ref[...] = encode(turned(total.T, -turn))


def call(kernel, name, out, inputs, scratch=(), specs=None, flops=0, moved=0, special=0):
    return pl.pallas_call(
        kernel,
        out_shape=tuple(jax.ShapeDtypeStruct(shape, dtype) for shape, dtype in out),
        in_specs=specs or [VMEM] * len(inputs),
        out_specs=(VMEM,) * len(out),
        scratch_shapes=list(scratch),
        compiler_params=pltpu.CompilerParams(vmem_limit_bytes=24 * MIB),
        cost_estimate=pl.CostEstimate(flops=flops, bytes_accessed=moved, transcendentals=special),
        name=name,
    )(*inputs)


def per_device(density, threshold_index, channel_width, sigma_table):
    planes, own_rows, nx = density.shape
    rows, cols = lax.axis_size("row"), lax.axis_size("col")
    ny = own_rows * rows
    cells = float(planes * ny * nx * cols)
    tall = VARIANTS * HALF
    turn = FIRST["row"] * own_rows

    xt, member, levels = call(
        bands_kernel,
        "bands",
        (((WIDTHS * HALF, 3 * HALF), BF16), ((32, 128), F32), ((24, 128), F32)),
        (sigma_table, channel_width, threshold_index),
        specs=[SMEM] * 3,
        flops=10_000_000,
        moved=2_500_000,
        special=500_000,
    )
    plane = regroup(density, "row").reshape(ny, nx)
    plane, xt, member, levels = lax.optimization_barrier((plane, xt, member, levels))
    right = lax.ppermute(plane, "col", [(i + 1, i) for i in range(cols - 1)])

    left = lax.ppermute(plane, "col", [(i, i + 1) for i in range(cols - 1)])
    b, own_rows_sum = call(
        partial(own_kernel, turn),
        "own",
        (((WIDTHS, tall, ny), F32), ((32, 128), F32)),
        (plane, xt, levels),
        scratch=(pltpu.VMEM((tall, ny), BF16), pltpu.VMEM((WIDTHS, tall, ny), F32)),
        flops=750_000_000,
        moved=7_000_000,
        special=100_000,
    )
    (part,) = call(
        partial(cross_kernel, turn),
        "cross",
        (((rows, 1, 128), F32),),
        (right, xt, levels, b, own_rows_sum),
        scratch=(pltpu.VMEM((32, 128), F32),),
        flops=250_000_000,
        moved=5_000_000,
        special=100_000,
    )
    part = regroup(part, "row")
    (part,) = call(gather_kernel, "regroup", (((cols, 1, 128), F32),), (part,))
    part = regroup(part, "col")

    (a,) = call(
        partial(along_kernel, turn),
        "along",
        (((WIDTHS, tall, ny), BF16),),
        (left, plane, right, xt, levels),
        scratch=(pltpu.VMEM((3 * HALF, ny), BF16),),
        flops=800_000_000,
        moved=4_000_000,
        special=300_000,
    )
    compliance, sensitivity = call(
        partial(combine_kernel, cells, turn),
        "combine",
        (((CHANNELS,), F32), ((ny, nx), BF16)),
        (part, member, a, plane, xt, levels),
        scratch=(pltpu.VMEM((VARIANTS, HALF, ny), F32),),
        flops=500_000_000,
        moved=5_000_000,
    )
    sensitivity = decode(regroup(sensitivity.reshape(planes, own_rows, nx), "row"))
    return compliance, sensitivity


def solution(mesh):
    in_specs = (P(None, "row", "col"), P(), P(), P())
    out_specs = (P(), P(None, "row", "col"))
    return jax.shard_map(
        per_device, mesh=mesh, in_specs=in_specs, out_specs=out_specs, check_vma=False
    )
```

```python
from functools import partial

import jax
import jax.numpy as jnp
from jax import lax
from jax.experimental import pallas as pl
from jax.experimental.pallas import tpu as pltpu
from jax.sharding import PartitionSpec as P

VARIANTS = 3
WIDTHS = 10
CHANNELS = 30
HALF = 128
SHARPNESS = 8.0
SPREAD_FLOOR = 0.0001

F32 = jnp.float32
BF16 = jnp.bfloat16
VMEM = pl.BlockSpec(memory_space=pltpu.VMEM)
SMEM = pl.BlockSpec(memory_space=pltpu.SMEM)
MIB = 1024 * 1024
SCALE = 1024.0
FIRST = {"row": 23, "col": 9}


def bands_kernel(sigma_ref, width_ref, index_ref, xt_ref, member_ref, level_ref):
    row = lax.broadcasted_iota(jnp.int32, (HALF, HALF), 0)
    col = lax.broadcasted_iota(jnp.int32, (HALF, HALF), 1)
    gap = col - row
    gap_f = gap.astype(F32)
    squares = ((gap_f - HALF) ** 2, gap_f * gap_f, (gap_f + HALF) ** 2)
    masks = (gap >= 0, None, gap <= 0)
    taps = lax.broadcasted_iota(jnp.int32, (1, HALF), 1).astype(F32) + 1.0
    for w in range(WIDTHS):
        sigma = jnp.full((1, HALF), sigma_ref[w], F32)
        scale = -1.0 / (2.0 * sigma * sigma)
        total = 1.0 + 2.0 * jnp.sum(jnp.exp(taps * taps * scale), axis=1, keepdims=True)
        inverse = 1.0 / total
        blocks = []
        for square, mask in zip(squares, masks):
            value = jnp.exp(square * scale) * inverse
            if mask is not None:
                value = jnp.where(mask, value, 0.0)
            blocks.append(value.astype(BF16))
        before, middle, after = blocks
        rows = slice(w * HALF, (w + 1) * HALF)
        xt_ref[rows, 0:HALF] = before
        xt_ref[rows, HALF : 2 * HALF] = middle
        xt_ref[rows, 2 * HALF : 3 * HALF] = after
    lane = lax.broadcasted_iota(jnp.int32, (1, 128), 1)
    for c in range(CHANNELS):
        pair = (c // WIDTHS) * WIDTHS + width_ref[c]
        member_ref[c : c + 1, :] = (lane == pair).astype(F32)
    member_ref[CHANNELS:32, :] = jnp.zeros((32 - CHANNELS, 128), F32)
    for v in range(VARIANTS):
        level = jnp.full((1, 128), index_ref[v].astype(F32) * (1.0 / 16.0), F32)
        low = jnp.tanh(SHARPNESS * level)
        high = jnp.tanh(SHARPNESS * (1.0 - level))
        level_ref[v : v + 1, :] = level
        level_ref[8 + v : 9 + v, :] = low
        level_ref[16 + v : 17 + v, :] = 1.0 / (low + high)


def regroup(x, axis):
    size = lax.axis_size(axis)
    order = [(FIRST[axis] + i) % size for i in range(size)]
    return lax.all_to_all(x, axis, split_axis=0, concat_axis=0, axis_index_groups=[order], tiled=True)


def turned(x, rows):
    rows %= x.shape[0]
    return x if rows == 0 else jnp.concatenate([x[-rows:], x[:-rows]], axis=0)


def columns(plane_ref, turn):
    return turned(plane_ref[...], turn).T


def encode(x):
    power = x * SCALE
    for _ in range(3):
        power = power * power
    return jnp.where(x < 0.0, -power, power).astype(BF16)


def decode(code):
    power = code.astype(F32)
    root = jnp.abs(power)
    for _ in range(3):
        root = jnp.sqrt(root)
    return jnp.where(power < 0.0, -root, root) * (1.0 / SCALE)


def column_to_row(column):
    rows = column.shape[0]
    at = lax.broadcasted_iota(jnp.int32, (rows, 128), 0) == lax.broadcasted_iota(jnp.int32, (rows, 128), 1)
    return jnp.sum(jnp.where(at, jnp.broadcast_to(column, (rows, 128)), 0.0), axis=0, keepdims=True)


def constants(level_ref, v, width):
    rows = [level_ref[8 * i + v : 8 * i + v + 1, :] for i in range(3)]
    return [jnp.concatenate([row] * (width // 128), axis=1) for row in rows]


def project(side, level, low, inverse):
    inner = jnp.tanh(SHARPNESS * (side - level))
    return ((low + inner) * inverse).astype(BF16), inner


def square_band(xt_ref, w):
    rows = pl.ds(w * HALF, HALF)
    return jnp.concatenate([xt_ref[rows, HALF : 3 * HALF], xt_ref[rows, 0 : 2 * HALF]], axis=0)


def own_kernel(turn, own_ref, xt_ref, level_ref, b_ref, rows_ref, p_ref, a_ref):
    ny = own_ref.shape[0]
    own = columns(own_ref, turn)
    for v in range(VARIANTS):
        level, low, inverse = constants(level_ref, v, ny)
        value, _ = project(own, level, low, inverse)
        p_ref[v * HALF : (v + 1) * HALF, :] = value
    rows_ref[...] = jnp.zeros_like(rows_ref)
    for v in range(VARIANTS):
        part = p_ref[v * HALF : (v + 1) * HALF, :]
        along = jnp.dot(xt_ref[:, HALF : 2 * HALF], part, preferred_element_type=F32)
        a_ref[:, v * HALF : (v + 1) * HALF, :] = along.reshape(WIDTHS, HALF, ny)
    for w in range(WIDTHS):
        b = jnp.dot(p_ref[...], square_band(xt_ref, w), preferred_element_type=F32)
        b_ref[w] = b
        product = a_ref[w] * b
        for v in range(VARIANTS):
            line = jnp.sum(product[v * HALF : (v + 1) * HALF, :], axis=0, keepdims=True)
            rows_ref[v * WIDTHS + w : v * WIDTHS + w + 1, :] = line[:, 0:128] + line[:, 128:256]


def cross_kernel(turn, right_ref, xt_ref, level_ref, b_ref, own_rows_ref, part_ref, rows_ref):
    ny = right_ref.shape[0]
    right = columns(right_ref, turn)
    rows_ref[...] = own_rows_ref[...]
    for v in range(VARIANTS):
        level, low, inverse = constants(level_ref, v, ny)
        value, _ = project(right, level, low, inverse)
        along = jnp.dot(xt_ref[:, 2 * HALF : 3 * HALF], value, preferred_element_type=F32)
        for w in range(WIDTHS):
            product = along[w * HALF : (w + 1) * HALF, :] * b_ref[w, v * HALF : (v + 1) * HALF, :]
            line = jnp.sum(product, axis=0, keepdims=True)
            k = v * WIDTHS + w
            rows_ref[k : k + 1, :] += 2.0 * (line[:, 0:128] + line[:, 128:256])
    sums = column_to_row(jnp.sum(rows_ref[...], axis=1, keepdims=True))
    part_ref[...] = jnp.broadcast_to(sums.reshape(1, 1, 128), part_ref.shape)


def along_kernel(turn, left_ref, own_ref, right_ref, xt_ref, level_ref, a_ref, p_ref):
    ny = left_ref.shape[0]
    left, own, right = [columns(ref, turn) for ref in (left_ref, own_ref, right_ref)]
    for v in range(VARIANTS):
        level, low, inverse = constants(level_ref, v, ny)
        p_ref[0:HALF, :] = project(left, level, low, inverse)[0]
        p_ref[HALF : 2 * HALF, :] = project(own, level, low, inverse)[0]
        p_ref[2 * HALF : 3 * HALF, :] = project(right, level, low, inverse)[0]
        along = jnp.dot(xt_ref[...], p_ref[...], preferred_element_type=F32).astype(BF16)
        a_ref[:, v * HALF : (v + 1) * HALF, :] = along.reshape(WIDTHS, HALF, ny)


def gather_kernel(in_ref, out_ref):
    total = jnp.sum(in_ref[...], axis=0, keepdims=True)
    out_ref[...] = jnp.broadcast_to(total, out_ref.shape)


def combine_kernel(cells, turn, sums_ref, member_ref, a_ref, own_ref, xt_ref, level_ref, compliance_ref, out_ref, total_ref):
    pairs = jnp.sum(sums_ref[...], axis=0) * (1.0 / cells)
    member = member_ref[...]
    compliance = jnp.sum(member * pairs, axis=1, keepdims=True)
    valid = lax.broadcasted_iota(jnp.int32, (32, 1), 0) < CHANNELS
    mean = jnp.sum(compliance, axis=0, keepdims=True) * (1.0 / CHANNELS)
    away = jnp.where(valid, compliance - mean, 0.0)
    spread = jnp.sqrt(jnp.sum(away * away, axis=0, keepdims=True) * (1.0 / CHANNELS) + SPREAD_FLOOR)
    weight = (1.0 + away / spread) * (2.0 / CHANNELS)
    per_pair = jnp.sum(member * weight, axis=0, keepdims=True)
    compliance_ref[...] = column_to_row(compliance)[0, :CHANNELS]
    for w in range(WIDTHS):
        field = jnp.dot(a_ref[w], square_band(xt_ref, w), preferred_element_type=F32)
        for v in range(VARIANTS):
            k = v * WIDTHS + w
            term = per_pair[:, k : k + 1] * field[v * HALF : (v + 1) * HALF, :]
            total_ref[v] = term if w == 0 else total_ref[v] + term
    own = columns(own_ref, turn)
    total = None
    for v in range(VARIANTS):
        level, low, inverse = constants(level_ref, v, own.shape[1])
        inner = jnp.tanh(SHARPNESS * (own - level))
        term = total_ref[v] * (SHARPNESS * (1.0 - inner * inner) * inverse)
        total = term if total is None else total + term
    out_ref[...] = encode(turned(total.T, -turn))


def call(kernel, name, out, inputs, scratch=(), specs=None, flops=0, moved=0, special=0):
    return pl.pallas_call(
        kernel,
        out_shape=tuple(jax.ShapeDtypeStruct(shape, dtype) for shape, dtype in out),
        in_specs=specs or [VMEM] * len(inputs),
        out_specs=(VMEM,) * len(out),
        scratch_shapes=list(scratch),
        compiler_params=pltpu.CompilerParams(vmem_limit_bytes=24 * MIB),
        cost_estimate=pl.CostEstimate(flops=flops, bytes_accessed=moved, transcendentals=special),
        name=name,
    )(*inputs)


def per_device(density, threshold_index, channel_width, sigma_table):
    planes, own_rows, nx = density.shape
    rows, cols = lax.axis_size("row"), lax.axis_size("col")
    ny = own_rows * rows
    cells = float(planes * ny * nx * cols)
    tall = VARIANTS * HALF
    turn = FIRST["row"] * own_rows

    xt, member, levels = call(
        bands_kernel,
        "bands",
        (((WIDTHS * HALF, 3 * HALF), BF16), ((32, 128), F32), ((24, 128), F32)),
        (sigma_table, channel_width, threshold_index),
        specs=[SMEM] * 3,
        flops=10_000_000,
        moved=2_500_000,
        special=500_000,
    )
    plane = regroup(density, "row").reshape(ny, nx)
    plane, xt, member, levels = lax.optimization_barrier((plane, xt, member, levels))
    right = lax.ppermute(plane, "col", [(i + 1, i) for i in range(cols - 1)])

    left = lax.ppermute(plane, "col", [(i, i + 1) for i in range(cols - 1)])
    b, own_rows_sum = call(
        partial(own_kernel, turn),
        "own",
        (((WIDTHS, tall, ny), F32), ((32, 128), F32)),
        (plane, xt, levels),
        scratch=(pltpu.VMEM((tall, ny), BF16), pltpu.VMEM((WIDTHS, tall, ny), F32)),
        flops=750_000_000,
        moved=7_000_000,
        special=100_000,
    )
    (part,) = call(
        partial(cross_kernel, turn),
        "cross",
        (((rows, 1, 128), F32),),
        (right, xt, levels, b, own_rows_sum),
        scratch=(pltpu.VMEM((32, 128), F32),),
        flops=250_000_000,
        moved=5_000_000,
        special=100_000,
    )
    part = regroup(part, "row")
    (part,) = call(gather_kernel, "regroup", (((cols, 1, 128), F32),), (part,))
    part = regroup(part, "col")

    (a,) = call(
        partial(along_kernel, turn),
        "along",
        (((WIDTHS, tall, ny), BF16),),
        (left, plane, right, xt, levels),
        scratch=(pltpu.VMEM((3 * HALF, ny), BF16),),
        flops=800_000_000,
        moved=4_000_000,
        special=300_000,
    )
    compliance, sensitivity = call(
        partial(combine_kernel, cells, turn),
        "combine",
        (((CHANNELS,), F32), ((ny, nx), BF16)),
        (part, member, a, plane, xt, levels),
        scratch=(pltpu.VMEM((VARIANTS, HALF, ny), F32),),
        flops=500_000_000,
        moved=5_000_000,
    )
    sensitivity = decode(regroup(sensitivity.reshape(planes, own_rows, nx), "row"))
    return compliance, sensitivity


def solution(mesh):
    in_specs = (P(None, "row", "col"), P(), P(), P())
    out_specs = (P(), P(None, "row", "col"))
    return jax.shard_map(
        per_device, mesh=mesh, in_specs=in_specs, out_specs=out_specs, check_vma=False
    )
```
